256 devices in a mesh: pole: 8 (over z_lo, y), row: 4 (over x), col: 8 (over z_hi, core).
Axes of the slice: x: 4, y: 4, z: 8 (z_hi: 4, z_lo: 2; z = z_hi * 2 + z_lo), core: 2. Of those that a mesh axis runs over, the one named last changes fastest.
Arguments:
- inverse: bfloat16 [8, 2, 8192, 8192], P('pole', None, None, ('row', 'col')), may hold values from -0.0625 to 0.0625
- factor: bfloat16 [8, 2, 8192, 768], P('pole', None, ('row', 'col')), may hold values from -1 to 1
- diag_inverse: bfloat16 [8, 2, 768, 256], P('pole', None, ('row', 'col')), may hold values from -6 to 6
- widths: int32 [3], replicated, may hold values from 1 to 256, 512 in all
- pattern: int32 [32, 3], replicated, may hold values 0 or 1
- owner: int32 [32], replicated, may hold values from 0 to 31, each once
- assign: int32 [8], P('pole'), may hold values from 0 to 19
- pole_weights: float32 [20, 2], replicated, may hold values from -4 to 4
Outputs:
- rho_panel: float32 [8192, 768], P(('row', 'col'))
- rho_diag: float32 [768, 256], P(('row', 'col'))
The draws below stay inside these ranges and needn't reach their ends.
Inputs may be any that keep to these rules, and one draw needn't show every extreme that they name: The widths sum to 512 and the largest is exactly 256. `owner`: each piece number appears once.
All inputs are finite; a program needn't handle non-finite values.
Results may differ from the reference program's by a relative error of at most 0.0027.
Values may be sent and summed in bfloat16 or wider, within the bound.
No kernel may reach another device: no remote copies, remote signals or barrier semaphores. Data moves between devices by JAX's collectives and lax.ppermute only.
A program may use at most 192 MiB of HBM per device.

```python
import math
import jax
import jax.numpy as jnp
import numpy as np
from jax import lax

B = 256
NA = 32
NK = 3
NPOLE = 20
P_SIZE = 8
N = 8192
M = 768
G = 32
N_ROW = 4
N_COL = 8


def touch_ends(values, own_key, smallest, largest):
    index_at = [jax.random.randint(jax.random.fold_in(own_key, axis), (), 0, length) for axis, length in enumerate(values.shape)]
    widest = values.shape.index(max(values.shape))
    neighbour = index_at[:widest] + [(index_at[widest] + 1) % values.shape[widest]] + index_at[widest + 1:]
    return values.at[tuple(index_at)].set(smallest).at[tuple(neighbour)].set(largest)


def shard_levels(own_key, shape, shards, smallest, largest):
    def one(axis_at, shards_of):
        heights = jax.random.uniform(jax.random.fold_in(jax.random.fold_in(own_key, 6), axis_at), (shards_of,), jnp.float32, smallest / len(shards), largest / len(shards))
        return jnp.repeat(jnp.exp(heights), shape[axis_at] // shards_of).reshape((-1,) + (1,) * (len(shape) - axis_at - 1))

    level = one(*shards[0])
    for cut in shards[1:]:
        level = level * one(*cut)
    return level


def profile(number_of, total, reach, slope):
    weights = [(1 << 20) // math.isqrt(grade ** slope) + 1 for grade in range(2, number_of + 1)]
    rest, given = total - reach - (number_of - 1), [1] * (number_of - 1)
    while rest > 0:
        free = [i for i in range(number_of - 1) if given[i] < reach]
        mass, budget = sum([weights[i] for i in free]), rest
        for i in free:
            extra = min(reach - given[i], max(1, budget * weights[i] // mass), rest)
            given[i] = given[i] + extra
            rest = rest - extra
    return np.array([reach] + given)


def uneven_parts(rng, number_of, total, most, skew):
    if number_of == 2:
        one = jax.random.randint(rng, (), max(1, total - most), min(most, total - 1) + 1)
        return jnp.stack([one, total - one])
    lengths = jnp.asarray(profile(number_of, total, most, skew), jnp.int32)
    twos = (number_of - 1) // 2
    donor, receiver = lengths[1:1 + 2 * twos:2], lengths[2:2 + 2 * twos:2]
    margin = jnp.minimum(donor - 1, most - receiver)
    passed = jax.random.randint(jax.random.fold_in(rng, 1), (twos,), 0, 1 << 20) % (margin + 1)
    lengths = lengths.at[1:1 + 2 * twos:2].set(donor - passed).at[2:2 + 2 * twos:2].set(receiver + passed)
    return lengths[jax.random.permutation(jax.random.fold_in(rng, 2), number_of)]


def centred(own_key, extent, deviation, reach, split=(), kind=jnp.bfloat16):
    array = jax.random.normal(own_key, extent, jnp.float32) * deviation
    if len(split) > 0:
        array = shard_levels(own_key, extent, split, -0.22, 0.18) * array
    return jnp.clip(array, min=-reach, max=reach).astype(kind)


def setup_inputs(seed: int = 0) -> dict:
    splits = jax.random.split(jax.random.key(seed), 9)
    return {
        "inverse": centred(splits[0], (P_SIZE, 2, N, N), (NA * B) ** -0.5, 0.0625, ((0, 8), (3, 32))),
        "factor": centred(splits[1], (P_SIZE, 2, N, M), 0.15, 1.0, ((0, 8), (2, 32))),
        "diag_inverse": centred(splits[2], (P_SIZE, 2, M, B), 1.0, 6.0, ((0, 8), (2, 32))),
        "widths": uneven_parts(splits[3], NK, 2 * NK * B // 3, B, 1).astype(jnp.int32),
        "pattern": touch_ends((jax.random.randint(splits[4], (NA, NK), 0, 3) < 2).astype(jnp.int32), jax.random.fold_in(splits[4], 1), 0, 1),
        "owner": jax.random.permutation(splits[5], G).astype(jnp.int32),
        "assign": touch_ends(jax.random.randint(splits[6], (P_SIZE,), 0, NPOLE), jax.random.fold_in(splits[6], 1), 0, NPOLE - 1).astype(jnp.int32),
        "pole_weights": centred(splits[7], (NPOLE, 2), 1.0, 4.0, (), jnp.float32),
    }


def plain_dot(left, right):
    return jnp.dot(left, right, preferred_element_type=jnp.float32)


def reference(inverse, factor, diag_inverse, widths, pattern, owner, assign, pole_weights):
    grid_count = N_ROW * N_COL
    total_rows = NA * B
    total_cols = NK * B
    piece_rows = total_rows // grid_count
    row_block = (jnp.arange(total_rows) // B).astype(jnp.int32)
    col_block = (jnp.arange(total_cols) // B).astype(jnp.int32)
    col_pos = (jnp.arange(total_cols) % B).astype(jnp.int32)
    col_live = (col_pos < widths[col_block]).astype(jnp.int32)
    keep = pattern[row_block][:, col_block] * col_live[None, :]
    masked = factor * keep.astype(jnp.bfloat16)[None, None]
    weights = pole_weights[assign]

    def one_pole(inputs):
        inv, panel, dinv, weight = inputs
        sum_real = plain_dot(inv[0].T, panel[0]) - plain_dot(inv[1].T, panel[1])
        sum_imag = plain_dot(inv[0].T, panel[1]) + plain_dot(inv[1].T, panel[0])
        x_real = -sum_real
        x_imag = -sum_imag
        panel_density = weight[0] * x_imag + weight[1] * x_real
        x_bf = jnp.stack([x_real, x_imag]).astype(jnp.bfloat16)
        own = panel.reshape(2, grid_count, piece_rows, total_cols)[:, owner].reshape(2, total_rows, total_cols)
        own_blocks = own.reshape(2, total_rows, NK, B).astype(jnp.float32)
        x_blocks = x_bf.reshape(2, total_rows, NK, B).astype(jnp.float32)
        part_real = jnp.einsum("nka,nkb->kab", own_blocks[0], x_blocks[0]) - jnp.einsum("nka,nkb->kab", own_blocks[1], x_blocks[1])
        part_imag = jnp.einsum("nka,nkb->kab", own_blocks[0], x_blocks[1]) + jnp.einsum("nka,nkb->kab", own_blocks[1], x_blocks[0])
        diag_real = dinv[0].astype(jnp.float32) - part_real.reshape(total_cols, B)
        diag_imag = dinv[1].astype(jnp.float32) - part_imag.reshape(total_cols, B)
        diag_density = weight[0] * diag_imag + weight[1] * diag_real
        return panel_density, diag_density

    panels, diags = lax.map(one_pole, (inverse, masked, diag_inverse, weights))
    return jnp.sum(panels, axis=0), jnp.sum(diags, axis=0)
```

```python
import jax
import jax.numpy as jnp
from jax import lax
from jax.experimental import pallas as pl
from jax.experimental.pallas import tpu as pltpu
from jax.sharding import PartitionSpec as P

NX, NZ, NC = 4, 4, 2
FIRST = 384
GRID = ("row", "col")


def place(x, z, c):
    return ((x % NX) * NZ + z % NZ) * NC + c % NC


def shift(value, dx, dz, dc):
    perm = [
        (place(x, z, c), place(x + dx, z + dz, c + dc))
        for x in range(NX)
        for z in range(NZ)
        for c in range(NC)
    ]
    return lax.ppermute(value, GRID, perm)


def ring(value, dx, dz):
    half = value.shape[0] // 2
    fwd = shift(value, dx, dz, 0)
    bwd = shift(value, -dx, -dz, 0)
    far_low = shift(fwd[:half], dx, dz, 0)
    far_high = shift(bwd[half:], -dx, -dz, 0)
    return value, fwd, bwd, far_low, far_high


def gemm_body(order_ref, a_ref, l_ref, acc_ref, out_ref):
    @pl.when(pl.program_id(0) == 0)
    def _():
        out_ref[...] = acc_ref[...]

    block = a_ref.shape[2]
    for i in range(2):
        out_ref[i * block : (i + 1) * block, :] += lax.dot_general(
            a_ref[i], l_ref[...], (((0,), (0,)), ((), ())), preferred_element_type=jnp.float32
        )


def gemm(order, inverse, panel, acc):
    block = inverse.shape[2]
    cols = panel.shape[1]
    steps = panel.shape[0] // block
    return pl.pallas_call(
        gemm_body,
        grid_spec=pltpu.PrefetchScalarGridSpec(
            num_scalar_prefetch=1,
            grid=(steps,),
            in_specs=[
                pl.BlockSpec((2, block, block), lambda j, order: (0, order[j], 0)),
                pl.BlockSpec((block, cols), lambda j, order: (j, 0)),
                pl.BlockSpec((2 * block, cols), lambda j, order: (0, 0)),
            ],
            out_specs=pl.BlockSpec((2 * block, cols), lambda j, order: (0, 0)),
        ),
        out_shape=jax.ShapeDtypeStruct((2 * block, cols), jnp.float32),
        input_output_aliases={3: 0},
        compiler_params=pltpu.CompilerParams(vmem_limit_bytes=32 * 1024 * 1024),
    )(order, inverse, panel, acc)


def dot(left, right):
    return jnp.dot(left, right, preferred_element_type=jnp.float32)


def local(inverse, factor, diag_inverse, widths, pattern, owner, assign, pole_weights):
    device = lax.axis_index(GRID)
    here_x, here_z, here_c = device // (NZ * NC), device // NC % NZ, device % NC
    poles = lax.axis_size("pole")
    block = diag_inverse.shape[3]
    blocks_k = widths.shape[0]
    total = factor.shape[3]
    live = 2 * block
    inverse = inverse[0]

    full = jnp.argmax(widths).astype(jnp.int32)
    one = jnp.where(full == 0, 1, 0)
    two = jnp.where(full == 2, 1, 2)
    split = widths[one]
    slot = jnp.arange(live, dtype=jnp.int32)
    slot_k = jnp.where(slot < block, full, jnp.where(slot < block + split, one, two))
    slot_at = jnp.where(
        slot < block, slot, jnp.where(slot < block + split, slot - block, slot - block - split)
    )
    source = slot_k * block + slot_at
    spread = jnp.arange(total, dtype=jnp.int32)[:, None] == source[None, :]
    kept = lax.dynamic_index_in_dim(pattern, device, 0, False)
    kept_slot = sum(jnp.where(slot_k == k, kept[k], 0) for k in range(blocks_k))
    pick = jnp.where(spread, kept_slot[None, :], 0).astype(jnp.bfloat16)
    spread = spread.astype(jnp.bfloat16)
    own = [dot(factor[0, i], pick).astype(jnp.bfloat16) for i in range(2)]
    first = jnp.concatenate([own[0][:, :FIRST], own[1][:, :FIRST]], 1)
    second = jnp.concatenate([own[0][:, FIRST:], own[1][:, FIRST:]], 1)

    def order_of(offsets):
        return jnp.stack(
            [place(here_x + ox, here_z + oz, here_c + oc) for ox, oz, oc in offsets]
        ).astype(jnp.int32)

    wanted = lax.dynamic_index_in_dim(owner, device, 0, False)

    def pick_own(picked, panel, order):
        for_row = jnp.argmax(order == wanted)
        rows = lax.dynamic_slice_in_dim(panel, for_row * block, block, 0)
        return jnp.where(jnp.any(order == wanted), rows, picked)

    far = 2
    across = ring(second, 1, 0)
    across = jnp.concatenate(across, 0)
    x_order = (0, -1, 1, far)
    z_order = (0, -1, 1, far)
    z0, zf, zb, zl, zh = ring(first, 0, 1)
    groups = [(z0, (0,)), (jnp.concatenate([zf, zb], 0), (-1, 1)), (jnp.concatenate([zl, zh], 0), (far,))]

    sum_first = jnp.zeros((2 * block, 2 * FIRST), jnp.float32)
    sum_second = jnp.zeros((2 * block, 2 * (live - FIRST)), jnp.float32)
    own_first = jnp.zeros((block, 2 * FIRST), jnp.bfloat16)
    own_second = jnp.zeros((block, 2 * (live - FIRST)), jnp.bfloat16)

    for piece, offsets_z in groups:
        panel = jnp.concatenate(ring(piece, 1, 0), 0)
        for plane in range(NC):
            held = shift(panel, 0, 0, 1) if plane else panel
            order = order_of([(ox, oz, plane) for ox in x_order for oz in offsets_z])
            sum_first = gemm(order, inverse, held, sum_first)
            own_first = pick_own(own_first, held, order)

    panel = jnp.concatenate(ring(across, 0, 1), 0)
    for plane in range(NC):
        held = shift(panel, 0, 0, 1) if plane else panel
        order = order_of([(ox, oz, plane) for oz in z_order for ox in x_order])
        sum_second = gemm(order, inverse, held, sum_second)
        own_second = pick_own(own_second, held, order)

    def quadrants(sums):
        cols = sums.shape[1] // 2
        return sums[:block, :cols], sums[:block, cols:], sums[block:, :cols], sums[block:, cols:]

    rr, ri, ir, ii = [jnp.concatenate(q, 1) for q in zip(quadrants(sum_first), quadrants(sum_second))]
    x_real, x_imag = ii - rr, -(ri + ir)
    weight = lax.dynamic_index_in_dim(pole_weights, assign[0], 0, False)
    panel_part = weight[0] * x_imag + weight[1] * x_real
    own_real = jnp.concatenate([own_first[:, :FIRST], own_second[:, : live - FIRST]], 1)
    own_imag = jnp.concatenate([own_first[:, FIRST:], own_second[:, live - FIRST :]], 1)

    def expand(value):
        return dot(value.astype(jnp.bfloat16), spread.T).astype(jnp.bfloat16)

    own_both = expand(jnp.concatenate([own_real, own_imag], 0))
    x_both = expand(jnp.concatenate([x_real, x_imag], 0))
    corrections = []
    for k in range(blocks_k):
        cut = slice(k * block, (k + 1) * block)
        lr, li = own_both[:block, cut], own_both[block:, cut]
        xr, xi = x_both[:block, cut], x_both[block:, cut]
        product = lax.dot_general(
            jnp.concatenate([lr, li], 0),
            jnp.concatenate(
                [jnp.concatenate([xi, xr], 0), jnp.concatenate([xr, -xi], 0)], 1
            ),
            (((0,), (0,)), ((), ())),
            preferred_element_type=jnp.float32,
        )
        corrections.append(weight[0] * product[:, :block] + weight[1] * product[:, block:])
    correction = jnp.concatenate(corrections, 0)
    inverse_diag = diag_inverse[0].astype(jnp.float32)
    own_diag = weight[0] * inverse_diag[1] + weight[1] * inverse_diag[0]
    pieces = NX * NZ * NC
    depth = total // pieces
    is_own = (jnp.arange(pieces) == device)[:, None, None]
    diag_part = jnp.where(is_own, own_diag[None], 0) - correction.reshape(pieces, depth, block)

    share = depth // poles * block
    sent = jnp.concatenate(
        [
            panel_part.reshape(poles, block // poles, live),
            diag_part.reshape(pieces, poles, share).transpose(1, 0, 2),
        ],
        2,
    ).astype(jnp.bfloat16)
    got = lax.all_to_all(sent, "pole", 0, 0, tiled=True).astype(jnp.float32).sum(0)
    panel_share, diag_share = got[:, :live], got[:, live:]
    diag_share = lax.all_to_all(diag_share, GRID, 0, 0, tiled=True).sum(0)
    both = jnp.concatenate([panel_share.reshape(-1), diag_share.reshape(-1)]).reshape(1, -1, 128)
    both = lax.all_to_all(
        jnp.broadcast_to(both, (poles,) + both.shape[1:]), "pole", 0, 0, tiled=True
    ).reshape(poles, -1)
    cut = block // poles * live
    panel_total = both[:, :cut].reshape(block, live)
    diag_total = both[:, cut:].reshape(depth, block)
    panel_out = jnp.dot(
        panel_total, spread.T.astype(jnp.float32), precision=lax.Precision.HIGHEST
    )
    return panel_out, diag_total


def solution(mesh):
    placed = (
        P("pole", None, None, GRID),
        P("pole", None, GRID, None),
        P("pole", None, GRID, None),
        P(),
        P(),
        P(),
        P("pole"),
        P(),
    )
    return jax.shard_map(
        local,
        mesh=mesh,
        in_specs=placed,
        out_specs=(P(GRID, None), P(GRID, None)),
        check_vma=False,
    )
```

```python
import functools

import jax
import jax.numpy as jnp
from jax import lax
from jax.experimental import pallas as pl
from jax.experimental.pallas import tpu as pltpu
from jax.sharding import PartitionSpec as P

NX, NZ, NC = 4, 4, 2
POLES = 8
B = 256
HALF = 128
GRID = ("row", "col")
MIB = 1024 * 1024
VMEM = pl.BlockSpec(memory_space=pltpu.VMEM)
SMEM = pl.BlockSpec(memory_space=pltpu.SMEM)
ANY = pl.BlockSpec(memory_space=pl.ANY)


def place(x, z, c):
    return ((x % NX) * NZ + z % NZ) * NC + c % NC


def shift(value, dx, dz, dc=0):
    perm = [
        (place(x, z, c), place(x + dx, z + dz, c + dc))
        for x in range(NX)
        for z in range(NZ)
        for c in range(NC)
    ]
    return lax.ppermute(value, GRID, perm)


def params(mib):
    return pltpu.CompilerParams(vmem_limit_bytes=mib * MIB)


def transposed_dot(left, right):
    return lax.dot_general(
        left, right, (((0,), (0,)), ((), ())), preferred_element_type=jnp.float32
    )


def layout(widths):
    full = jnp.where(widths[0] == B, 0, jnp.where(widths[1] == B, 1, 2))
    one = jnp.where(full == 0, 1, 0)
    two = jnp.where(full == 2, 1, 2)
    return full, one, two, widths[one]


def moved(split):
    at_row = lax.broadcasted_iota(jnp.int32, (B, B), 0)
    at_col = lax.broadcasted_iota(jnp.int32, (B, B), 1)
    return (at_row + split == at_col).astype(jnp.float32).astype(jnp.bfloat16)


def prepare_body(device, widths, pattern, factor, top, rest, give):
    dev = device[0]
    full, one, two, split = layout(widths)

    def cut(i, k):
        return factor[i, :, pl.ds(pl.multiple_of(k * B, B), B)]

    def kept(value, k):
        keep = (pattern[dev, k] > 0).astype(jnp.float32)
        return (value.astype(jnp.float32) * keep).astype(jnp.bfloat16)

    col = lax.broadcasted_iota(jnp.int32, (B, B), 1)
    move = moved(split)
    large, small = [], []
    for i in range(2):
        large.append(kept(cut(i, full), full))
        late = jnp.dot(cut(i, two), move, preferred_element_type=jnp.float32)
        keep_one = (pattern[dev, one] > 0).astype(jnp.float32)
        keep_two = (pattern[dev, two] > 0).astype(jnp.float32)
        both = jnp.where(col < split, cut(i, one).astype(jnp.float32) * keep_one, late * keep_two)
        small.append(both.astype(jnp.bfloat16))

    def store(mine, other):
        for i in range(2):
            at = slice(i * B, (i + 1) * B)
            top[:, at] = mine[i][:HALF]
            rest[:, at] = mine[i][HALF:]
            give[:, at] = other[i]

    @pl.when(dev % NC == 0)
    def _():
        store(large, small)

    @pl.when(dev % NC == 1)
    def _():
        store(small, large)


def prepare(device, widths, pattern, factor):
    half = jax.ShapeDtypeStruct((HALF, 2 * B), jnp.bfloat16)
    return pl.pallas_call(
        prepare_body,
        in_specs=[SMEM, SMEM, SMEM, VMEM],
        out_specs=[VMEM] * 3,
        out_shape=[half, half, jax.ShapeDtypeStruct((B, 2 * B), jnp.bfloat16)],
        compiler_params=params(16),
    )(device, widths, pattern, factor)


def gemm_body(segments, chunks, has_acc, *refs):
    device, own, sib = refs[:3]
    acc = refs[3] if has_acc else None
    dev = device[0]
    core, here_x, here_z = dev % NC, dev // (NZ * NC), dev // NC % NZ
    pieces = refs[3 + has_acc : 3 + has_acc + len(segments)]
    out, a_buf, l_buf, a_sem, l_sem = refs[3 + has_acc + len(segments) :]
    waits = []
    at, s = 0, 0
    for i, rows in enumerate(segments):
        total = sum(size for *_, size in rows)
        copy = pltpu.make_async_copy(pieces[i], l_buf.at[pl.ds(at, total)], l_sem.at[i])
        copy.start()
        mine = [copy]
        for ox, oz, same, low, n in rows:
            block = place(here_x + ox, here_z + oz, core if same else 1 - core)
            source = pl.ds(pl.multiple_of(block * B + low, HALF), n)
            for j, a in enumerate((own, sib)):
                copy = pltpu.make_async_copy(
                    a.at[:, source], a_buf.at[2 * j : 2 * j + 2, pl.ds(at, n)], a_sem.at[j, s]
                )
                copy.start()
                mine.append(copy)
            at, s = at + n, s + 1
        waits.append((mine, at))
    begin, done = 0, 0
    for chunk in chunks:
        for i in range(done, done + chunk):
            for copy in waits[i][0]:
                copy.wait()
        end = waits[done + chunk - 1][1]
        for q in range(4):
            part = transposed_dot(a_buf[q, begin:end], l_buf[begin:end])
            rows = slice(q * B, (q + 1) * B)
            if begin:
                out[rows] += part
            elif has_acc:
                out[rows] = acc[rows] + part
            else:
                out[rows] = part
        begin, done = end, done + chunk


def gemm(device, own, sib, acc, pieces, segments):
    depth = sum(size for rows in segments for *_, size in rows)
    count = sum(map(len, segments))
    has_acc = acc is not None
    return pl.pallas_call(
        functools.partial(gemm_body, segments, (2, 2), has_acc),
        in_specs=[SMEM, ANY, ANY] + [VMEM] * has_acc + [ANY] * len(pieces),
        out_specs=VMEM,
        out_shape=jax.ShapeDtypeStruct((4 * B, 2 * B), jnp.float32),
        scratch_shapes=[
            pltpu.VMEM((4, depth, B), jnp.bfloat16),
            pltpu.VMEM((depth, 2 * B), jnp.bfloat16),
            pltpu.SemaphoreType.DMA((2, count)),
            pltpu.SemaphoreType.DMA((len(pieces),)),
        ],
        compiler_params=params(32),
    )(device, own, sib, *([acc] if has_acc else []), *pieces)


def finish_body(sources, *refs):
    device, widths, owner, assign, weights, acc, dinv = refs[:7]
    pieces = refs[7 : 7 + len(sources)]
    sent, own, diag, sem = refs[7 + len(sources) :]
    dev = device[0]
    core = dev % NC
    here_x, here_z = dev // (NZ * NC), dev // NC % NZ
    full, one, two, split = layout(widths)

    waits = []
    for j in range(2):
        block = dev if j == 0 else dev + 1 - 2 * core
        want = owner[block]
        chip, same = want // NC, want % NC == core
        for h in range(2):
            target = own.at[pl.ds(j * B + h * HALF, HALF)]
            for piece, rows in zip(pieces, sources, strict=True):
                for at, is_same, part, (ox, oz) in rows:
                    if part != h:
                        continue
                    here = place(here_x + ox, here_z + oz, 0) // NC

                    @pl.when((here == chip) & (same == is_same))
                    def _(piece=piece, at=at, target=target, j=j, h=h):
                        pltpu.make_async_copy(
                            piece.at[pl.ds(at, HALF)], target, sem.at[j, h]
                        ).start()

            waits.append(
                pltpu.make_async_copy(pieces[0].at[pl.ds(0, HALF)], target, sem.at[j, h])
            )

    wr, wi = weights[assign[0], 0], weights[assign[0], 1]
    parts = []
    for j in range(2):
        top, low = acc[2 * j * B : (2 * j + 1) * B], acc[(2 * j + 1) * B : (2 * j + 2) * B]
        x_real = low[:, B:] - top[:, :B]
        x_imag = -(top[:, B:] + low[:, :B])
        density = (wr * x_imag + wi * x_real).astype(jnp.bfloat16)
        for p in range(POLES):
            rows = B // POLES
            sent[p, j * rows : (j + 1) * rows] = density[p * rows : (p + 1) * rows]
        parts.append((x_real.astype(jnp.bfloat16), x_imag.astype(jnp.bfloat16)))
    for copy in waits:
        copy.wait()
    real = imag = 0
    for j in range(2):
        l_real, l_imag = own[j * B : (j + 1) * B, :B], own[j * B : (j + 1) * B, B:]
        x_real, x_imag = parts[j]
        real += transposed_dot(l_real, x_real) - transposed_dot(l_imag, x_imag)
        imag += transposed_dot(l_real, x_imag) + transposed_dot(l_imag, x_real)
    both = wr * imag + wi * real

    cut = jnp.where(core == 0, B, split)
    at_row = lax.broadcasted_iota(jnp.int32, (B, B), 0)
    at_col = lax.broadcasted_iota(jnp.int32, (B, B), 1)
    before = jnp.where((at_row < cut) & (at_col < cut), both, 0)
    after = jnp.where((at_row >= cut) & (at_col >= cut), both, 0).astype(jnp.bfloat16)
    move = moved(cut)
    after = lax.dot_general(move, after, (((1,), (0,)), ((), ())), preferred_element_type=jnp.float32)
    after = lax.dot_general(
        after.astype(jnp.bfloat16), move, (((1,), (1,)), ((), ())), preferred_element_type=jnp.float32
    )
    diag[...] = jnp.zeros_like(diag)
    first = jnp.where(core == 0, full, one)
    second = jnp.where(core == 0, one, two)
    depth = dinv.shape[1]
    mine = pl.ds(pl.multiple_of(dev * depth, 8), depth)
    weighted = wr * dinv[1] + wi * dinv[0]
    for h in range(B // HALF):
        cols = slice(h * HALF, (h + 1) * HALF)
        diag[h, pl.ds(pl.multiple_of(first * B, B), B)] = -before[:, cols]
        diag[h, pl.ds(pl.multiple_of(second * B, B), B)] = -after[:, cols]
        diag[h, mine] += weighted[:, cols]
        for p in range(POLES):
            sent[p, 2 * B // POLES :, cols] = diag[
                h, pl.ds(p, diag.shape[1] // POLES, stride=POLES)
            ].astype(jnp.bfloat16)


def finish(device, widths, owner, assign, weights, acc, dinv, pieces, sources, total):
    return pl.pallas_call(
        functools.partial(finish_body, sources),
        in_specs=[SMEM] * 5 + [VMEM] * 2 + [ANY] * len(pieces),
        out_specs=VMEM,
        out_shape=jax.ShapeDtypeStruct((POLES, (2 * B + total) // POLES, B), jnp.bfloat16),
        scratch_shapes=[
            pltpu.VMEM((2 * B, 2 * B), jnp.bfloat16),
            pltpu.VMEM((B // HALF, total, HALF), jnp.float32),
            pltpu.SemaphoreType.DMA((2, 2)),
        ],
        compiler_params=params(32),
    )(device, widths, owner, assign, weights, acc, dinv, *pieces)


def spread_body(device, widths, got, panel, diag):
    core = device[0] % NC
    full, one, two, split = layout(widths)
    rows = B // POLES
    col = lax.broadcasted_iota(jnp.int32, (rows, B), 1)
    for p in range(POLES):
        out = slice(p * rows, (p + 1) * rows)
        mine, other = got[p, :rows], got[p, rows : 2 * rows]
        large = jnp.where(core == 0, mine, other)
        small = jnp.where(core == 0, other, mine)
        panel[out, pl.ds(pl.multiple_of(full * B, B), B)] = large
        panel[out, pl.ds(pl.multiple_of(one * B, B), B)] = jnp.where(col < split, small, 0)
        late = pltpu.roll(small, B - split, 1)
        panel[out, pl.ds(pl.multiple_of(two * B, B), B)] = jnp.where(col < B - split, late, 0)
        for t in range(diag.shape[0] // POLES):
            diag[t * POLES + p : t * POLES + p + 1] = got[p, 2 * rows + t : 2 * rows + t + 1]


def spread(device, widths, got, total, depth):
    return pl.pallas_call(
        spread_body,
        in_specs=[SMEM, SMEM, VMEM],
        out_specs=[VMEM, VMEM],
        out_shape=[
            jax.ShapeDtypeStruct((B, total), jnp.float32),
            jax.ShapeDtypeStruct((depth, B), jnp.float32),
        ],
        compiler_params=params(16),
    )(device, widths, got)


def local(inverse, factor, diag_inverse, widths, pattern, owner, assign, pole_weights):
    dev = lax.axis_index(GRID)
    device = dev[None].astype(jnp.int32)
    total = factor.shape[3]
    depth = diag_inverse.shape[2]
    own_inverse = inverse[0]
    top, rest, give = prepare(device, widths, pattern, factor[0])
    taken = shift(give, 0, 0, 1)
    sib_inverse = shift(own_inverse, 0, 0, 1)

    pieces, sources = [], []

    def multiply(acc, held, offsets, kind):
        parts = ((True, HALF, HALF),) if kind else ((True, 0, HALF), (False, 0, B))
        segments = []
        for piece, some in zip(held, offsets, strict=True):
            rows, listed, at = [], [], 0
            for ox, oz in some:
                for same, low, size in parts:
                    rows.append((ox, oz, same, low, size))
                    for k in range(0, size, HALF):
                        listed.append((at + k, same, (low + k) // HALF, (ox, oz)))
                    at += size
            pieces.append(piece)
            sources.append(tuple(listed))
            segments.append(tuple(rows))
        return gemm(device, own_inverse, sib_inverse, acc, held, tuple(segments))

    def after(values, *others):
        values, _ = lax.optimization_barrier((values, others))
        return values

    def along_x(oz):
        return [[(ox, oz)] for ox in (0, -1, 1, 2)]

    rest_f, rest_b = shift(rest, 1, 0), shift(rest, -1, 0)
    main = jnp.concatenate([top, taken], 0)
    zf, zb = shift(main, 0, 1), shift(main, 0, -1)
    rest_far = shift(rest_f, 1, 0)
    main_f, main_b = shift(main, 1, 0), shift(main, -1, 0)
    across = jnp.concatenate([rest, rest_f, rest_b, rest_far], 0)
    main_far = shift(main_b, -1, 0)
    z_far = shift(zf, 0, 1)
    zff, zbb = shift(zf, 1, 0), shift(zb, -1, 0)
    zfb, zbf = shift(zf, -1, 0), shift(zb, 1, 0)
    across = after(across, zf, zb)
    across_b = shift(across, 0, -1)
    acc = multiply(None, (main, main_f, main_b, main_far), along_x(0), 0)
    z_far, acc = after((z_far, acc), zff, zbb)
    far_f, far_b = shift(z_far, 1, 0), shift(z_far, -1, 0)
    zff, zbb, across, acc = after((zff, zbb, across, acc), z_far)
    zf_far, zb_far = shift(zff, 1, 0), shift(zbb, -1, 0)
    across_f = shift(across, 0, 1)
    across_b, acc = after((across_b, acc), zf_far)
    across_far = shift(across_b, 0, -1)
    acc = multiply(acc, (zf, zff, zfb, zf_far), along_x(-1), 0)
    far_f, acc = after((far_f, acc), zb_far)
    far_far = shift(far_f, 1, 0)
    acc = multiply(acc, (zb, zbf, zbb, zb_far), along_x(1), 0)
    across_far, acc = after((across_far, acc), across_f)
    acc = multiply(
        acc,
        (across, across_f, across_b, across_far),
        [[(ox, oz) for ox in (0, -1, 1, 2)] for oz in (0, -1, 1, 2)],
        1,
    )
    acc = multiply(acc, (z_far, far_f, far_b, far_far), along_x(2), 0)

    sent = finish(
        device, widths, owner, assign, pole_weights, acc,
        diag_inverse[0].astype(jnp.float32), pieces, tuple(sources), total,
    )

    got = lax.all_to_all(sent, "pole", 0, 0, tiled=True).astype(jnp.float32).sum(0)
    rows = B // POLES
    other = shift(got[rows : 2 * rows], 0, 0, 1)
    share = depth // POLES
    diag = got[2 * rows :].reshape(NX * NZ * NC, share * B)
    diag = lax.all_to_all(diag, GRID, 0, 0, tiled=True).sum(0).reshape(share, B)
    diag = jnp.pad(diag, ((0, 8 - share), (0, 0)))
    both = jnp.concatenate([got[:rows], other, diag], 0)
    both = lax.all_to_all(
        jnp.broadcast_to(both[None], (POLES,) + both.shape), "pole", 0, 0, tiled=True
    )
    return tuple(spread(device, widths, both, total, depth))


def solution(mesh):
    placed = (
        P("pole", None, None, GRID),
        P("pole", None, GRID, None),
        P("pole", None, GRID, None),
        P(),
        P(),
        P(),
        P("pole"),
        P(),
    )
    return jax.shard_map(
        local,
        mesh=mesh,
        in_specs=placed,
        out_specs=(P(GRID, None), P(GRID, None)),
        check_vma=False,
    )
```

```python
import functools

import jax
import jax.numpy as jnp
from jax import lax
from jax.experimental import pallas as pl
from jax.experimental.pallas import tpu as pltpu
from jax.sharding import PartitionSpec as P

NX, NZ, NC = 4, 4, 2
POLES = 8
B = 256
HALF = 128
GRID = ("row", "col")
MIB = 1024 * 1024
LIMIT = 20
VMEM = pl.BlockSpec(memory_space=pltpu.VMEM)
SMEM = pl.BlockSpec(memory_space=pltpu.SMEM)
ANY = pl.BlockSpec(memory_space=pl.ANY)
HBM = pl.BlockSpec(memory_space=pltpu.HBM)


def place(x, z, c):
    return ((x % NX) * NZ + z % NZ) * NC + c % NC


def shift(value, dx, dz, dc=0):
    perm = [
        (place(x, z, c), place(x + dx, z + dz, c + dc))
        for x in range(NX)
        for z in range(NZ)
        for c in range(NC)
    ]
    return lax.ppermute(value, GRID, perm)


def params(mib):
    return pltpu.CompilerParams(vmem_limit_bytes=mib * MIB)


def transposed_dot(left, right):
    return lax.dot_general(
        left, right, (((0,), (0,)), ((), ())), preferred_element_type=jnp.float32
    )


def layout(widths):
    full = jnp.where(widths[0] == B, 0, jnp.where(widths[1] == B, 1, 2))
    one = jnp.where(full == 0, 1, 0)
    two = jnp.where(full == 2, 1, 2)
    return full, one, two, widths[one]


def moved(split):
    at_row = lax.broadcasted_iota(jnp.int32, (B, B), 0)
    at_col = lax.broadcasted_iota(jnp.int32, (B, B), 1)
    return (at_row + split == at_col).astype(jnp.float32).astype(jnp.bfloat16)


def prepare_body(device, widths, pattern, factor, top, rest, give):
    dev = device[0]
    full, one, two, split = layout(widths)

    def cut(i, k):
        return factor[i, :, pl.ds(pl.multiple_of(k * B, B), B)]

    def kept(value, k):
        keep = (pattern[dev, k] > 0).astype(jnp.float32)
        return (value.astype(jnp.float32) * keep).astype(jnp.bfloat16)

    col = lax.broadcasted_iota(jnp.int32, (B, B), 1)
    move = moved(split)
    large, small = [], []
    for i in range(2):
        large.append(kept(cut(i, full), full))
        late = jnp.dot(cut(i, two), move, preferred_element_type=jnp.float32)
        keep_one = (pattern[dev, one] > 0).astype(jnp.float32)
        keep_two = (pattern[dev, two] > 0).astype(jnp.float32)
        both = jnp.where(col < split, cut(i, one).astype(jnp.float32) * keep_one, late * keep_two)
        small.append(both.astype(jnp.bfloat16))

    def store(mine, other):
        for i in range(2):
            at = slice(i * B, (i + 1) * B)
            top[:, at] = mine[i][:HALF]
            rest[:, at] = mine[i][HALF:]
            give[:, at] = other[i]

    @pl.when(dev % NC == 0)
    def _():
        store(large, small)

    @pl.when(dev % NC == 1)
    def _():
        store(small, large)


def prepare(device, widths, pattern, factor):
    half = jax.ShapeDtypeStruct((HALF, 2 * B), jnp.bfloat16)
    return pl.pallas_call(
        prepare_body,
        in_specs=[SMEM, SMEM, SMEM, VMEM],
        out_specs=[VMEM] * 3,
        out_shape=[half, half, jax.ShapeDtypeStruct((B, 2 * B), jnp.bfloat16)],
        compiler_params=params(16),
    )(device, widths, pattern, factor)


def gemm_body(segments, chunks, has_acc, *refs):
    device, own, sib = refs[:3]
    acc = refs[3] if has_acc else None
    dev = device[0]
    core, here_x, here_z = dev % NC, dev // (NZ * NC), dev // NC % NZ
    pieces = refs[3 + has_acc : 3 + has_acc + len(segments)]
    out, a_buf, l_buf, a_sem, l_sem = refs[3 + has_acc + len(segments) :]
    waits = []
    at, s = 0, 0
    for i, rows in enumerate(segments):
        total = sum(size for *_, size in rows)
        copy = pltpu.make_async_copy(pieces[i], l_buf.at[pl.ds(at, total)], l_sem.at[i])
        copy.start()
        mine = [copy]
        for ox, oz, same, low, n in rows:
            block = place(here_x + ox, here_z + oz, core if same else 1 - core)
            source = pl.ds(pl.multiple_of(block * B + low, HALF), n)
            for j, a in enumerate((own, sib)):
                copy = pltpu.make_async_copy(
                    a.at[:, source], a_buf.at[2 * j : 2 * j + 2, pl.ds(at, n)], a_sem.at[j, s]
                )
                copy.start()
                mine.append(copy)
            at, s = at + n, s + 1
        waits.append((mine, at))
    begin, done = 0, 0
    for chunk in chunks:
        for i in range(done, done + chunk):
            for copy in waits[i][0]:
                copy.wait()
        end = waits[done + chunk - 1][1]
        for q in range(4):
            part = transposed_dot(a_buf[q, begin:end], l_buf[begin:end])
            rows = slice(q * B, (q + 1) * B)
            if begin:
                out[rows] += part
            elif has_acc:
                out[rows] = acc[rows] + part
            else:
                out[rows] = part
        begin, done = end, done + chunk


def gemm(device, own, sib, acc, pieces, segments):
    depth = sum(size for rows in segments for *_, size in rows)
    count = sum(map(len, segments))
    has_acc = acc is not None
    return pl.pallas_call(
        functools.partial(gemm_body, segments, (2, 2), has_acc),
        in_specs=[SMEM, HBM, HBM] + [VMEM] * has_acc + [ANY] * len(pieces),
        out_specs=VMEM,
        out_shape=jax.ShapeDtypeStruct((4 * B, 2 * B), jnp.float32),
        scratch_shapes=[
            pltpu.VMEM((4, depth, B), jnp.bfloat16),
            pltpu.VMEM((depth, 2 * B), jnp.bfloat16),
            pltpu.SemaphoreType.DMA((2, count)),
            pltpu.SemaphoreType.DMA((len(pieces),)),
        ],
        compiler_params=params(LIMIT),
    )(device, own, sib, *([acc] if has_acc else []), *pieces)


def finish_body(sources, *refs):
    device, widths, owner, assign, weights, acc, dinv = refs[:7]
    pieces = refs[7 : 7 + len(sources)]
    shared, *parts_out, own, diag, weighted, sem = refs[7 + len(sources) :]
    dev, pole = device[0], device[1]
    core = dev % NC
    here_x, here_z = dev // (NZ * NC), dev // NC % NZ
    full, one, two, split = layout(widths)

    waits = []
    for j in range(2):
        block = dev if j == 0 else dev + 1 - 2 * core
        want = owner[block]
        chip, same = want // NC, want % NC == core
        for h in range(2):
            target = own.at[pl.ds(j * B + h * HALF, HALF)]
            for piece, rows in zip(pieces, sources, strict=True):
                for at, is_same, part, (ox, oz) in rows:
                    if part != h:
                        continue
                    here = place(here_x + ox, here_z + oz, 0) // NC

                    @pl.when((here == chip) & (same == is_same))
                    def _(piece=piece, at=at, target=target, j=j, h=h):
                        pltpu.make_async_copy(
                            piece.at[pl.ds(at, HALF)], target, sem.at[j, h]
                        ).start()

            waits.append(
                pltpu.make_async_copy(pieces[0].at[pl.ds(0, HALF)], target, sem.at[j, h])
            )

    wr, wi = weights[assign[0], 0], weights[assign[0], 1]
    parts = []
    for j in range(2):
        top, low = acc[2 * j * B : (2 * j + 1) * B], acc[(2 * j + 1) * B : (2 * j + 2) * B]
        x_real = low[:, B:] - top[:, :B]
        x_imag = -(top[:, B:] + low[:, :B])
        weighted[...] = (wr * x_imag + wi * x_real).astype(jnp.bfloat16)
        for d in range(POLES):
            rows = pl.ds(pl.multiple_of((pole ^ d) * (B // POLES), B // POLES), B // POLES)
            parts_out[d][j * (B // POLES) : (j + 1) * (B // POLES)] = weighted[rows]
        parts.append((x_real.astype(jnp.bfloat16), x_imag.astype(jnp.bfloat16)))
    for copy in waits:
        copy.wait()
    real = imag = 0
    for j in range(2):
        l_real, l_imag = own[j * B : (j + 1) * B, :B], own[j * B : (j + 1) * B, B:]
        x_real, x_imag = parts[j]
        real += transposed_dot(l_real, x_real) - transposed_dot(l_imag, x_imag)
        imag += transposed_dot(l_real, x_imag) + transposed_dot(l_imag, x_real)
    both = wr * imag + wi * real

    cut = jnp.where(core == 0, B, split)
    at_row = lax.broadcasted_iota(jnp.int32, (B, B), 0)
    at_col = lax.broadcasted_iota(jnp.int32, (B, B), 1)
    before = jnp.where((at_row < cut) & (at_col < cut), both, 0)
    after = jnp.where((at_row >= cut) & (at_col >= cut), both, 0).astype(jnp.bfloat16)
    move = moved(cut)
    after = lax.dot_general(move, after, (((1,), (0,)), ((), ())), preferred_element_type=jnp.float32)
    after = lax.dot_general(
        after.astype(jnp.bfloat16), move, (((1,), (1,)), ((), ())), preferred_element_type=jnp.float32
    )
    diag[...] = jnp.zeros_like(diag)
    first = jnp.where(core == 0, full, one)
    second = jnp.where(core == 0, one, two)
    diag[pl.ds(pl.multiple_of(first * B, B), B)] = -before
    diag[pl.ds(pl.multiple_of(second * B, B), B)] = -after
    depth = dinv.shape[1]
    mine = pl.ds(pl.multiple_of(dev * depth, 8), depth)
    diag[mine] += wr * dinv[1] + wi * dinv[0]
    shared[...] = diag[...].astype(jnp.bfloat16)


def finish(device, widths, owner, assign, weights, acc, dinv, pieces, sources, total):
    return pl.pallas_call(
        functools.partial(finish_body, sources),
        in_specs=[SMEM] * 5 + [VMEM] * 2 + [ANY] * len(pieces),
        out_specs=[VMEM] * (1 + POLES),
        out_shape=[
            jax.ShapeDtypeStruct((n, B), jnp.bfloat16)
            for n in (total,) + (2 * B // POLES,) * POLES
        ],
        scratch_shapes=[
            pltpu.VMEM((2 * B, 2 * B), jnp.bfloat16),
            pltpu.VMEM((total, B), jnp.float32),
            pltpu.VMEM((B, B), jnp.bfloat16),
            pltpu.SemaphoreType.DMA((2, 2)),
        ],
        compiler_params=params(LIMIT),
    )(device, widths, owner, assign, weights, acc, dinv, *pieces)


def spread_body(device, widths, got, panel, diag):
    core = device[0] % NC
    full, one, two, split = layout(widths)
    rows = B // POLES
    col = lax.broadcasted_iota(jnp.int32, (rows, B), 1)
    for p in range(POLES):
        out = slice(p * rows, (p + 1) * rows)
        mine, other = got[p, :rows], got[p, rows : 2 * rows]
        large = jnp.where(core == 0, mine, other)
        small = jnp.where(core == 0, other, mine)
        panel[out, pl.ds(pl.multiple_of(full * B, B), B)] = large
        panel[out, pl.ds(pl.multiple_of(one * B, B), B)] = jnp.where(col < split, small, 0)
        late = pltpu.roll(small, B - split, 1)
        panel[out, pl.ds(pl.multiple_of(two * B, B), B)] = jnp.where(col < B - split, late, 0)
    diag[...] = sum(got[p, 2 * rows :] for p in range(POLES))


def spread(device, widths, got, total, depth):
    return pl.pallas_call(
        spread_body,
        in_specs=[SMEM, SMEM, VMEM],
        out_specs=[VMEM, VMEM],
        out_shape=[
            jax.ShapeDtypeStruct((B, total), jnp.float32),
            jax.ShapeDtypeStruct((depth, B), jnp.float32),
        ],
        compiler_params=params(16),
    )(device, widths, got)


def local(inverse, factor, diag_inverse, widths, pattern, owner, assign, pole_weights):
    dev = lax.axis_index(GRID)
    device = jnp.stack([dev, lax.axis_index("pole")]).astype(jnp.int32)
    total = factor.shape[3]
    depth = diag_inverse.shape[2]
    own_inverse = pltpu.with_memory_space_constraint(inverse[0], pltpu.HBM)
    top, rest, give = prepare(device, widths, pattern, factor[0])
    taken = shift(give, 0, 0, 1)
    pieces, sources = [], []

    def multiply(acc, held, offsets, kind):
        parts = ((True, HALF, HALF),) if kind else ((True, 0, HALF), (False, 0, B))
        segments = []
        for piece, some in zip(held, offsets, strict=True):
            rows, listed, at = [], [], 0
            for ox, oz in some:
                for same, low, size in parts:
                    rows.append((ox, oz, same, low, size))
                    for k in range(0, size, HALF):
                        listed.append((at + k, same, (low + k) // HALF, (ox, oz)))
                    at += size
            pieces.append(piece)
            sources.append(tuple(listed))
            segments.append(tuple(rows))
        return gemm(device, own_inverse, sib_inverse, acc, held, tuple(segments))

    def after(values, *others):
        values, _ = lax.optimization_barrier((values, others))
        return values

    def along_x(oz):
        return [[(ox, oz)] for ox in (0, -1, 1, 2)]

    rest_f, rest_b = shift(rest, 1, 0), shift(rest, -1, 0)
    main = jnp.concatenate([top, taken], 0)
    rest_f, rest_b = after((rest_f, rest_b), main)
    zf, zb = shift(main, 0, 1), shift(main, 0, -1)
    rest_far = shift(rest_f, 1, 0)
    main_x = after(main, rest_f, rest_b)
    main_f, main_b = shift(main_x, 1, 0), shift(main_x, -1, 0)
    across = jnp.concatenate([rest, rest_f, rest_b, rest_far], 0)
    sib_inverse = shift(after(inverse[0], rest_far), 0, 0, 1)
    sib_inverse = pltpu.with_memory_space_constraint(sib_inverse, pltpu.HBM)
    main_far = shift(main_b, -1, 0)
    z_far = shift(zf, 0, 1)
    across_b = shift(after(across, zf, zb), 0, -1)
    zff, zbb = shift(zf, 1, 0), shift(zb, -1, 0)
    zf_late, zb_late = after((zf, zb), main_far)
    zfb, zbf = shift(zf_late, -1, 0), shift(zb_late, 1, 0)
    acc = multiply(None, (main, main_f, main_b, main_far), along_x(0), 0)
    z_far, acc = after((z_far, acc), zff, zbb)
    far_f, far_b = shift(z_far, 1, 0), shift(z_far, -1, 0)
    across_f = shift(after(across, z_far), 0, 1)
    zf_far, zb_far = shift(zff, 1, 0), shift(zbb, -1, 0)
    across_far = shift(across_b, 0, -1)
    acc = multiply(acc, (zf, zff, zfb, zf_far), along_x(-1), 0)
    acc = multiply(acc, (zb, zbf, zbb, zb_far), along_x(1), 0)
    far_f, acc = after((far_f, acc))
    far_far = shift(far_f, 1, 0)
    acc = multiply(
        acc,
        (across, across_f, across_b, across_far),
        [[(ox, oz) for ox in (0, -1, 1, 2)] for oz in (0, -1, 1, 2)],
        1,
    )
    acc = multiply(acc, (z_far, far_f, far_b, far_far), along_x(2), 0)

    shared, *parts = finish(
        device, widths, owner, assign, pole_weights, acc,
        diag_inverse[0].astype(jnp.float32), pieces, tuple(sources), total,
    )

    shared = shared.reshape(NX * NZ * NC, depth, B)
    shared = lax.all_to_all(shared, GRID, 0, 0, tiled=True)
    got = [
        lax.ppermute(part, "pole", [(p, p ^ d) for p in range(POLES)]) if d else part
        for d, part in enumerate(parts)
    ]
    got = sum(part.astype(jnp.float32) for part in got)
    rows = B // POLES
    other = shift(got[rows:], 0, 0, 1)
    diag = shared.astype(jnp.float32).sum(0)
    both = jnp.concatenate([got[:rows], other, diag], 0)
    both = lax.all_to_all(
        jnp.broadcast_to(both[None], (POLES,) + both.shape), "pole", 0, 0, tiled=True
    )
    return tuple(spread(device, widths, both, total, depth))


def solution(mesh):
    placed = (
        P("pole", None, None, GRID),
        P("pole", None, GRID, None),
        P("pole", None, GRID, None),
        P(),
        P(),
        P(),
        P("pole"),
        P(),
    )
    return jax.shard_map(
        local,
        mesh=mesh,
        in_specs=placed,
        out_specs=(P(GRID, None), P(GRID, None)),
        check_vma=False,
    )
```

```python
import functools

import jax
import jax.numpy as jnp
from jax import lax
from jax.experimental import pallas as pl
from jax.experimental.pallas import tpu as pltpu
from jax.sharding import PartitionSpec as P

NX, NZ, NC = 4, 4, 2
POLES = 8
B = 256
TOP = 128
SIZES = (TOP, B - TOP)
GRID = ("row", "col")
MIB = 1024 * 1024
LIMIT = 20
VMEM = pl.BlockSpec(memory_space=pltpu.VMEM)
SMEM = pl.BlockSpec(memory_space=pltpu.SMEM)
ANY = pl.BlockSpec(memory_space=pl.ANY)
HBM = pl.BlockSpec(memory_space=pltpu.HBM)


def place(x, z, c):
    return ((x % NX) * NZ + z % NZ) * NC + c % NC


def shift(value, dx, dz, dc=0):
    perm = [
        (place(x, z, c), place(x + dx, z + dz, c + dc))
        for x in range(NX)
        for z in range(NZ)
        for c in range(NC)
    ]
    return lax.ppermute(value, GRID, perm)


def alternate(fwd, bwd, core, dx, dz):
    perm = [
        (place(x, z, c), place(x + (dx if c == 0 else -dx), z + (dz if c == 0 else -dz), c))
        for x in range(NX)
        for z in range(NZ)
        for c in range(NC)
    ]
    return lax.ppermute(jnp.where(core == 0, fwd, bwd), GRID, perm)


def side(z, core):
    return 1 - 2 * ((z + core) % 2)


def pair(value, turn):
    perm = [
        (place(x, z, c), place(x, z + turn * side(z, c), c))
        for x in range(NX)
        for z in range(NZ)
        for c in range(NC)
    ]
    return lax.ppermute(value, GRID, perm)


def params(mib):
    return pltpu.CompilerParams(vmem_limit_bytes=mib * MIB)


def transposed_dot(left, right):
    return lax.dot_general(
        left, right, (((0,), (0,)), ((), ())), preferred_element_type=jnp.float32
    )


def layout(widths):
    full = jnp.where(widths[0] == B, 0, jnp.where(widths[1] == B, 1, 2))
    one = jnp.where(full == 0, 1, 0)
    two = jnp.where(full == 2, 1, 2)
    return full, one, two, widths[one]


def moved(split):
    at_row = lax.broadcasted_iota(jnp.int32, (B, B), 0)
    at_col = lax.broadcasted_iota(jnp.int32, (B, B), 1)
    return (at_row + split == at_col).astype(jnp.float32).astype(jnp.bfloat16)


def prepare_body(device, widths, pattern, factor, top, rest, give):
    dev = device[0]
    full, one, two, split = layout(widths)

    def cut(i, k):
        return factor[i, :, pl.ds(pl.multiple_of(k * B, B), B)]

    def kept(value, k):
        keep = (pattern[dev, k] > 0).astype(jnp.float32)
        return (value.astype(jnp.float32) * keep).astype(jnp.bfloat16)

    col = lax.broadcasted_iota(jnp.int32, (B, B), 1)
    move = moved(split)
    large, small = [], []
    for i in range(2):
        large.append(kept(cut(i, full), full))
        late = jnp.dot(cut(i, two), move, preferred_element_type=jnp.float32)
        keep_one = (pattern[dev, one] > 0).astype(jnp.float32)
        keep_two = (pattern[dev, two] > 0).astype(jnp.float32)
        both = jnp.where(col < split, cut(i, one).astype(jnp.float32) * keep_one, late * keep_two)
        small.append(both.astype(jnp.bfloat16))

    def store(mine, other):
        for i in range(2):
            at = slice(i * B, (i + 1) * B)
            top[:, at] = mine[i][:TOP]
            rest[:, at] = mine[i][TOP:]
            give[:, at] = other[i]

    @pl.when(dev % NC == 0)
    def _():
        store(large, small)

    @pl.when(dev % NC == 1)
    def _():
        store(small, large)


def prepare(device, widths, pattern, factor):
    shapes = [jax.ShapeDtypeStruct((n, 2 * B), jnp.bfloat16) for n in SIZES + (B,)]
    return pl.pallas_call(
        prepare_body,
        in_specs=[SMEM, SMEM, SMEM, VMEM],
        out_specs=[VMEM] * 3,
        out_shape=shapes,
        compiler_params=params(16),
    )(device, widths, pattern, factor)


def gemm_body(segments, has_acc, *refs):
    device, own, sib = refs[:3]
    acc = refs[3] if has_acc else None
    pieces = refs[3 + has_acc : 3 + has_acc + len(segments)]
    out, *scratch = refs[3 + has_acc + len(segments) :]
    waits = gemm_fetch(segments, device[0], own, sib, pieces, *scratch)
    gemm_sum(waits, acc, out, *scratch[:2])


def gemm_fetch(segments, dev, own, sib, pieces, a_buf, l_buf, a_sem, l_sem):
    core, here_x, here_z = dev % NC, dev // (NZ * NC), dev // NC % NZ
    waits = []
    at, s = 0, 0
    for i, rows in enumerate(segments):
        total = sum(size for *_, size in rows)
        copy = pltpu.make_async_copy(pieces[i], l_buf.at[pl.ds(at, total)], l_sem.at[i])
        copy.start()
        mine = [copy]
        for ox, oz, sided, same, low, n in rows:
            go = oz * side(here_z, core) if sided else oz
            block = place(here_x + ox, here_z + go, core if same else 1 - core)
            source = pl.ds(pl.multiple_of(block * B + low, 32), n)
            for j, a in enumerate((own, sib)):
                copy = pltpu.make_async_copy(
                    a.at[:, source], a_buf.at[2 * j : 2 * j + 2, pl.ds(at, n)], a_sem.at[j, s]
                )
                copy.start()
                mine.append(copy)
            at, s = at + n, s + 1
        waits.append((mine, at))
    return waits


def gemm_sum(waits, acc, out, a_buf, l_buf):
    begin, done, chunk = 0, 0, 2
    while done < len(waits):
        for i in range(done, done + chunk):
            for copy in waits[i][0]:
                copy.wait()
        end = waits[done + chunk - 1][1]
        for q in range(4):
            part = transposed_dot(a_buf[q, begin:end], l_buf[begin:end])
            rows = slice(q * B, (q + 1) * B)
            if begin:
                out[rows] += part
            elif acc is not None:
                out[rows] = acc[rows] + part
            else:
                out[rows] = part
        begin, done = end, done + chunk


def gemm_scratch(segments):
    depth = sum(size for rows in segments for *_, size in rows)
    return [
        pltpu.VMEM((4, depth, B), jnp.bfloat16),
        pltpu.VMEM((depth, 2 * B), jnp.bfloat16),
        pltpu.SemaphoreType.DMA((2, sum(map(len, segments)))),
        pltpu.SemaphoreType.DMA((len(segments),)),
    ]


def gemm(device, own, sib, acc, pieces, segments):
    has_acc = acc is not None
    return pl.pallas_call(
        functools.partial(gemm_body, segments, has_acc),
        in_specs=[SMEM, HBM, HBM] + [VMEM] * has_acc + [ANY] * len(pieces),
        out_specs=VMEM,
        out_shape=jax.ShapeDtypeStruct((4 * B, 2 * B), jnp.float32),
        scratch_shapes=gemm_scratch(segments),
        compiler_params=params(LIMIT),
    )(device, own, sib, *([acc] if has_acc else []), *pieces)


def finish_body(sources, segments, *refs):
    device, widths, owner, assign, weights, acc, dinv, own_inverse, sib_inverse = refs[:9]
    pieces = refs[9 : 9 + len(sources)]
    shared = refs[9 + len(sources)]
    parts_out = refs[10 + len(sources) : 10 + len(sources) + POLES]
    total, own, diag, weighted, sem, *scratch = refs[10 + len(sources) + POLES :]
    last = pieces[len(sources) - len(segments) :]
    fetched = gemm_fetch(segments, device[0], own_inverse, sib_inverse, last, *scratch)
    dev, pole = device[0], device[1]
    core = dev % NC
    here_x, here_z = dev // (NZ * NC), dev // NC % NZ
    full, one, two, split = layout(widths)

    waits = []
    for j in range(2):
        block = dev if j == 0 else dev + 1 - 2 * core
        want = owner[block]
        chip, same = want // NC, want % NC == core
        for h in range(2):
            size = SIZES[h]
            target = own.at[pl.ds(j * B + h * TOP, size)]
            for piece, rows in zip(pieces, sources, strict=True):
                for at, is_same, part, (ox, oz, sided) in rows:
                    if part != h:
                        continue
                    go = oz * side(here_z, core) if sided else oz
                    here = place(here_x + ox, here_z + go, 0) // NC

                    @pl.when((here == chip) & (same == is_same))
                    def _(piece=piece, at=at, size=size, target=target, j=j, h=h):
                        pltpu.make_async_copy(
                            piece.at[pl.ds(at, size)], target, sem.at[j, h]
                        ).start()

            waits.append(
                pltpu.make_async_copy(pieces[0].at[pl.ds(0, size)], target, sem.at[j, h])
            )

    gemm_sum(fetched, acc, total, *scratch[:2])
    acc = total
    wr, wi = weights[assign[0], 0], weights[assign[0], 1]
    parts = []
    for j in range(2):
        top, low = acc[2 * j * B : (2 * j + 1) * B], acc[(2 * j + 1) * B : (2 * j + 2) * B]
        x_real = low[:, B:] - top[:, :B]
        x_imag = -(top[:, B:] + low[:, :B])
        weighted[...] = (wr * x_imag + wi * x_real).astype(jnp.bfloat16)
        for d in range(POLES):
            rows = pl.ds(pl.multiple_of((pole ^ d) * (B // POLES), B // POLES), B // POLES)
            parts_out[d][j * (B // POLES) : (j + 1) * (B // POLES)] = weighted[rows]
        parts.append((x_real.astype(jnp.bfloat16), x_imag.astype(jnp.bfloat16)))
    for copy in waits:
        copy.wait()
    real = imag = 0
    for j in range(2):
        l_real, l_imag = own[j * B : (j + 1) * B, :B], own[j * B : (j + 1) * B, B:]
        x_real, x_imag = parts[j]
        real += transposed_dot(l_real, x_real) - transposed_dot(l_imag, x_imag)
        imag += transposed_dot(l_real, x_imag) + transposed_dot(l_imag, x_real)
    both = wr * imag + wi * real

    cut = jnp.where(core == 0, B, split)
    at_row = lax.broadcasted_iota(jnp.int32, (B, B), 0)
    at_col = lax.broadcasted_iota(jnp.int32, (B, B), 1)
    before = jnp.where((at_row < cut) & (at_col < cut), both, 0)
    after = jnp.where((at_row >= cut) & (at_col >= cut), both, 0).astype(jnp.bfloat16)
    move = moved(cut)
    after = lax.dot_general(move, after, (((1,), (0,)), ((), ())), preferred_element_type=jnp.float32)
    after = lax.dot_general(
        after.astype(jnp.bfloat16), move, (((1,), (1,)), ((), ())), preferred_element_type=jnp.float32
    )
    diag[...] = jnp.zeros_like(diag)
    first = jnp.where(core == 0, full, one)
    second = jnp.where(core == 0, one, two)
    diag[pl.ds(pl.multiple_of(first * B, B), B)] = -before
    diag[pl.ds(pl.multiple_of(second * B, B), B)] = -after
    depth = dinv.shape[1]
    mine = pl.ds(pl.multiple_of(dev * depth, 8), depth)
    diag[mine] += wr * dinv[1] + wi * dinv[0]
    shared[...] = diag[...].astype(jnp.bfloat16)


def finish(
    device, widths, owner, assign, weights, acc, dinv, own, sib, pieces, sources, segments, total
):
    return pl.pallas_call(
        functools.partial(finish_body, sources, segments),
        in_specs=[SMEM] * 5 + [VMEM] * 2 + [HBM] * 2 + [ANY] * len(pieces),
        out_specs=[VMEM] * (1 + POLES),
        out_shape=[
            jax.ShapeDtypeStruct((n, B), jnp.bfloat16)
            for n in (total,) + (2 * B // POLES,) * POLES
        ],
        scratch_shapes=[
            pltpu.VMEM((4 * B, 2 * B), jnp.float32),
            pltpu.VMEM((2 * B, 2 * B), jnp.bfloat16),
            pltpu.VMEM((total, B), jnp.float32),
            pltpu.VMEM((B, B), jnp.bfloat16),
            pltpu.SemaphoreType.DMA((2, 2)),
            *gemm_scratch(segments),
        ],
        compiler_params=params(LIMIT),
    )(device, widths, owner, assign, weights, acc, dinv, own, sib, *pieces)


def spread_body(device, widths, got, panel, diag):
    core = device[0] % NC
    full, one, two, split = layout(widths)
    rows = B // POLES
    col = lax.broadcasted_iota(jnp.int32, (rows, B), 1)
    for p in range(POLES):
        out = slice(p * rows, (p + 1) * rows)
        mine, other = got[p, :rows], got[p, rows : 2 * rows]
        large = jnp.where(core == 0, mine, other)
        small = jnp.where(core == 0, other, mine)
        panel[out, pl.ds(pl.multiple_of(full * B, B), B)] = large
        panel[out, pl.ds(pl.multiple_of(one * B, B), B)] = jnp.where(col < split, small, 0)
        late = pltpu.roll(small, B - split, 1)
        panel[out, pl.ds(pl.multiple_of(two * B, B), B)] = jnp.where(col < B - split, late, 0)
    diag[...] = sum(got[p, 2 * rows :] for p in range(POLES))


def spread(device, widths, got, total, depth):
    return pl.pallas_call(
        spread_body,
        in_specs=[SMEM, SMEM, VMEM],
        out_specs=[VMEM, VMEM],
        out_shape=[
            jax.ShapeDtypeStruct((B, total), jnp.float32),
            jax.ShapeDtypeStruct((depth, B), jnp.float32),
        ],
        compiler_params=params(16),
    )(device, widths, got)


def local(inverse, factor, diag_inverse, widths, pattern, owner, assign, pole_weights):
    dev = lax.axis_index(GRID)
    device = jnp.stack([dev, lax.axis_index("pole")]).astype(jnp.int32)
    total = factor.shape[3]
    depth = diag_inverse.shape[2]
    own_inverse = pltpu.with_memory_space_constraint(inverse[0], pltpu.HBM)
    top, rest, give = prepare(device, widths, pattern, factor[0])
    taken = shift(give, 0, 0, 1)
    pieces, sources = [], []

    def listing(held, offsets, kind):
        parts = ((True, TOP, B - TOP),) if kind else ((True, 0, TOP), (False, 0, B))
        segments = []
        for piece, some in zip(held, offsets, strict=True):
            rows, listed, at = [], [], 0
            for ox, oz, sided in some:
                for same, low, size in parts:
                    rows.append((ox, oz, sided, same, low, size))
                    for h, begin in enumerate((0, TOP)):
                        if low <= begin < low + size:
                            listed.append((at + begin - low, same, h, (ox, oz, sided)))
                    at += size
            pieces.append(pltpu.with_memory_space_constraint(piece, pltpu.HBM))
            sources.append(tuple(listed))
            segments.append(tuple(rows))
        return tuple(segments)

    def after(values, *others):
        values, _ = lax.optimization_barrier((values, others))
        return values

    orders = (0, -1, 1, 2)
    core = dev % NC
    rest_f, rest_b = shift(rest, 1, 0), shift(rest, -1, 0)
    main = jnp.concatenate([top, taken], 0)
    rest_f, rest_b = after((rest_f, rest_b), main)
    zf, zb = shift(main, 0, 1), shift(main, 0, -1)
    rest_far = shift(rest_f, 1, 0)
    main_x = after(main, rest_f, rest_b)
    main_f, main_b = shift(main_x, 1, 0), shift(main_x, -1, 0)
    across = jnp.concatenate([rest, rest_f, rest_b, rest_far], 0)
    sib_inverse = shift(after(inverse[0], main), 0, 0, 1)
    sib_inverse = pltpu.with_memory_space_constraint(sib_inverse, pltpu.HBM)
    main_far = shift(main_b, -1, 0)
    z_far = shift(zf, 0, 1)
    across_b = shift(after(across, zf, zb), 0, -1)
    zff, zbb = shift(zf, 1, 0), shift(zb, -1, 0)
    zf_late, zb_late = after((zf, zb), main_far)
    zfb, zbf = shift(zf_late, -1, 0), shift(zb_late, 1, 0)
    held = (main, main_f, main_b, main_far)
    segments = listing(held, [[(ox, 0, False)] for ox in orders], 0)
    acc = gemm(device, own_inverse, sib_inverse, None, held, segments)
    z_far, acc = after((z_far, acc), zff, zbb)
    far_f, far_b = shift(z_far, 1, 0), shift(z_far, -1, 0)
    across_f = shift(after(across, z_far), 0, 1)
    zf_far, zb_far = shift(zff, 1, 0), shift(zbb, -1, 0)
    across_far = shift(across_b, 0, -1)
    held = (zf, zff, zfb, zf_far)
    segments = listing(held, [[(ox, -1, False)] for ox in orders], 0)
    acc = gemm(device, own_inverse, sib_inverse, acc, held, segments)
    held = (zb, zbf, zbb, zb_far)
    segments = listing(held, [[(ox, 1, False)] for ox in orders], 0)
    acc = gemm(device, own_inverse, sib_inverse, acc, held, segments)
    far_f, acc = after((far_f, acc))
    far_far = shift(far_f, 1, 0)
    held = (across, across_f, across_b, across_far)
    segments = listing(held, [[(ox, oz, False) for ox in orders] for oz in orders], 1)
    held = (z_far, far_f, far_b, far_far)
    segments += listing(held, [[(ox, 2, False)] for ox in orders], 0)

    shared, *parts = finish(
        device, widths, owner, assign, pole_weights, acc,
        diag_inverse[0].astype(jnp.float32), own_inverse, sib_inverse,
        pieces, tuple(sources), segments, total,
    )

    shared = shared.reshape(NX * NZ * NC, depth, B)
    shared = lax.all_to_all(shared, GRID, 0, 0, tiled=True)
    got = [
        lax.ppermute(part, "pole", [(p, p ^ d) for p in range(POLES)]) if d else part
        for d, part in enumerate(parts)
    ]
    got = sum(part.astype(jnp.float32) for part in got)
    rows = B // POLES
    other = shift(got[rows:], 0, 0, 1)
    diag = shared.astype(jnp.float32).sum(0)
    both = jnp.concatenate([got[:rows], other, diag], 0)
    both = lax.all_to_all(
        jnp.broadcast_to(both[None], (POLES,) + both.shape), "pole", 0, 0, tiled=True
    )
    return tuple(spread(device, widths, both, total, depth))


def solution(mesh):
    placed = (
        P("pole", None, None, GRID),
        P("pole", None, GRID, None),
        P("pole", None, GRID, None),
        P(),
        P(),
        P(),
        P("pole"),
        P(),
    )
    return jax.shard_map(
        local,
        mesh=mesh,
        in_specs=placed,
        out_specs=(P(GRID, None), P(GRID, None)),
        check_vma=False,
    )
```

```python
import functools

import jax
import jax.numpy as jnp
from jax import lax
from jax.experimental import pallas as pl
from jax.experimental.pallas import tpu as pltpu
from jax.sharding import PartitionSpec as P

NX, NZ, NC = 4, 4, 2
POLES, NY = 8, 4
B = 256
TOP = 128
SIZES = (TOP, B - TOP)
GRID = ("row", "col")
MIB = 1024 * 1024
LIMIT = 20
VMEM = pl.BlockSpec(memory_space=pltpu.VMEM)
SMEM = pl.BlockSpec(memory_space=pltpu.SMEM)
ANY = pl.BlockSpec(memory_space=pl.ANY)
HBM = pl.BlockSpec(memory_space=pltpu.HBM)


def place(x, z, c):
    return ((x % NX) * NZ + z % NZ) * NC + c % NC


def shift(value, dx, dz, dc=0):
    perm = [
        (place(x, z, c), place(x + dx, z + dz, c + dc))
        for x in range(NX)
        for z in range(NZ)
        for c in range(NC)
    ]
    return lax.ppermute(value, GRID, perm)


def alternate(fwd, bwd, core, dx, dz):
    perm = [
        (place(x, z, c), place(x + (dx if c == 0 else -dx), z + (dz if c == 0 else -dz), c))
        for x in range(NX)
        for z in range(NZ)
        for c in range(NC)
    ]
    return lax.ppermute(jnp.where(core == 0, fwd, bwd), GRID, perm)


def side(z, core):
    return 1 - 2 * ((z + core) % 2)


def pair(value, turn):
    perm = [
        (place(x, z, c), place(x, z + turn * side(z, c), c))
        for x in range(NX)
        for z in range(NZ)
        for c in range(NC)
    ]
    return lax.ppermute(value, GRID, perm)


def params(mib):
    return pltpu.CompilerParams(vmem_limit_bytes=mib * MIB)


def transposed_dot(left, right):
    return lax.dot_general(
        left, right, (((0,), (0,)), ((), ())), preferred_element_type=jnp.float32
    )


def layout(widths):
    full = jnp.where(widths[0] == B, 0, jnp.where(widths[1] == B, 1, 2))
    one = jnp.where(full == 0, 1, 0)
    two = jnp.where(full == 2, 1, 2)
    return full, one, two, widths[one]


def moved(split):
    at_row = lax.broadcasted_iota(jnp.int32, (B, B), 0)
    at_col = lax.broadcasted_iota(jnp.int32, (B, B), 1)
    return (at_row + split == at_col).astype(jnp.float32).astype(jnp.bfloat16)


def pass_on(*values, flops):
    n = len(values)
    return pl.pallas_call(
        lambda *refs: None,
        in_specs=[ANY] * n,
        out_specs=[ANY] * n,
        out_shape=[jax.ShapeDtypeStruct(v.shape, v.dtype) for v in values],
        input_output_aliases={i: i for i in range(n)},
        cost_estimate=pl.CostEstimate(flops=flops, transcendentals=0, bytes_accessed=0),
    )(*values)


def prepare_body(device, widths, pattern, factor, top, rest, give):
    dev = device[0]
    full, one, two, split = layout(widths)

    def cut(i, k):
        return factor[i, :, pl.ds(pl.multiple_of(k * B, B), B)]

    def kept(value, k):
        keep = (pattern[dev, k] > 0).astype(jnp.float32)
        return (value.astype(jnp.float32) * keep).astype(jnp.bfloat16)

    col = lax.broadcasted_iota(jnp.int32, (B, B), 1)
    move = moved(split)
    large, small = [], []
    for i in range(2):
        large.append(kept(cut(i, full), full))
        late = jnp.dot(cut(i, two), move, preferred_element_type=jnp.float32)
        keep_one = (pattern[dev, one] > 0).astype(jnp.float32)
        keep_two = (pattern[dev, two] > 0).astype(jnp.float32)
        both = jnp.where(col < split, cut(i, one).astype(jnp.float32) * keep_one, late * keep_two)
        small.append(both.astype(jnp.bfloat16))

    def store(mine, other):
        for i in range(2):
            at = slice(i * B, (i + 1) * B)
            top[:, at] = mine[i][:TOP]
            rest[:, at] = mine[i][TOP:]
            give[:, at] = other[i]

    @pl.when(dev % NC == 0)
    def _():
        store(large, small)

    @pl.when(dev % NC == 1)
    def _():
        store(small, large)


def prepare(device, widths, pattern, factor):
    shapes = [jax.ShapeDtypeStruct((n, 2 * B), jnp.bfloat16) for n in SIZES + (B,)]
    return pl.pallas_call(
        prepare_body,
        in_specs=[SMEM, SMEM, SMEM, VMEM],
        out_specs=[VMEM] * 3,
        out_shape=shapes,
        compiler_params=params(16),
    )(device, widths, pattern, factor)


def gemm_body(segments, has_acc, *refs):
    device, own, sib = refs[:3]
    acc = refs[3] if has_acc else None
    pieces = refs[3 + has_acc : 3 + has_acc + len(segments)]
    out, *scratch = refs[3 + has_acc + len(segments) :]
    waits = gemm_fetch(segments, device[0], own, sib, pieces, *scratch)
    gemm_sum(waits, acc, out, *scratch[:2])


def gemm_fetch(segments, dev, own, sib, pieces, a_buf, l_buf, a_sem, l_sem):
    core, here_x, here_z = dev % NC, dev // (NZ * NC), dev // NC % NZ
    waits = []
    at, s = 0, 0
    for i, rows in enumerate(segments):
        total = sum(size for *_, size in rows)
        copy = pltpu.make_async_copy(pieces[i], l_buf.at[pl.ds(at, total)], l_sem.at[i])
        copy.start()
        mine = [copy]
        for ox, oz, sided, same, low, n in rows:
            go = oz * side(here_z, core) if sided else oz
            block = place(here_x + ox, here_z + go, core if same else 1 - core)
            source = pl.ds(pl.multiple_of(block * B + low, 32), n)
            for j, a in enumerate((own, sib)):
                copy = pltpu.make_async_copy(
                    a.at[:, source], a_buf.at[2 * j : 2 * j + 2, pl.ds(at, n)], a_sem.at[j, s]
                )
                copy.start()
                mine.append(copy)
            at, s = at + n, s + 1
        waits.append((mine, at))
    return waits


def gemm_sum(waits, acc, out, a_buf, l_buf):
    begin, done, chunk = 0, 0, 2
    while done < len(waits):
        for i in range(done, done + chunk):
            for copy in waits[i][0]:
                copy.wait()
        end = waits[done + chunk - 1][1]
        for q in range(4):
            part = transposed_dot(a_buf[q, begin:end], l_buf[begin:end])
            rows = slice(q * B, (q + 1) * B)
            if begin:
                out[rows] += part
            elif acc is not None:
                out[rows] = acc[rows] + part
            else:
                out[rows] = part
        begin, done = end, done + chunk


def gemm_scratch(segments):
    depth = sum(size for rows in segments for *_, size in rows)
    return [
        pltpu.VMEM((4, depth, B), jnp.bfloat16),
        pltpu.VMEM((depth, 2 * B), jnp.bfloat16),
        pltpu.SemaphoreType.DMA((2, sum(map(len, segments)))),
        pltpu.SemaphoreType.DMA((len(segments),)),
    ]


def gemm(device, own, sib, acc, pieces, segments):
    has_acc = acc is not None
    return pl.pallas_call(
        functools.partial(gemm_body, segments, has_acc),
        in_specs=[SMEM, HBM, HBM] + [VMEM] * has_acc + [ANY] * len(pieces),
        out_specs=VMEM,
        out_shape=jax.ShapeDtypeStruct((4 * B, 2 * B), jnp.float32),
        scratch_shapes=gemm_scratch(segments),
        compiler_params=params(LIMIT),
    )(device, own, sib, *([acc] if has_acc else []), *pieces)


def finish_body(sources, segments, *refs):
    device, widths, owner, assign, weights, acc, dinv, own_inverse, sib_inverse = refs[:9]
    pieces = refs[9 : 9 + len(sources)]
    mine_out, other_out, over_out, *parts_out = refs[9 + len(sources) : 12 + len(sources) + NY]
    total, own, diag, weighted, sem, *scratch = refs[12 + len(sources) + NY :]
    last = pieces[len(sources) - len(segments) :]
    fetched = gemm_fetch(segments, device[0], own_inverse, sib_inverse, last, *scratch)
    dev, pole = device[0], device[1]
    core = dev % NC
    here_x, here_z = dev // (NZ * NC), dev // NC % NZ
    full, one, two, split = layout(widths)

    waits = []
    for j in range(2):
        block = dev if j == 0 else dev + 1 - 2 * core
        want = owner[block]
        chip, same = want // NC, want % NC == core
        for h in range(2):
            size = SIZES[h]
            target = own.at[pl.ds(j * B + h * TOP, size)]
            for piece, rows in zip(pieces, sources, strict=True):
                for at, is_same, part, (ox, oz, sided) in rows:
                    if part != h:
                        continue
                    go = oz * side(here_z, core) if sided else oz
                    here = place(here_x + ox, here_z + go, 0) // NC

                    @pl.when((here == chip) & (same == is_same))
                    def _(piece=piece, at=at, size=size, target=target, j=j, h=h):
                        pltpu.make_async_copy(
                            piece.at[pl.ds(at, size)], target, sem.at[j, h]
                        ).start()

            waits.append(
                pltpu.make_async_copy(pieces[0].at[pl.ds(0, size)], target, sem.at[j, h])
            )

    gemm_sum(fetched, acc, total, *scratch[:2])
    acc = total
    wr, wi = weights[assign[0], 0], weights[assign[0], 1]
    parts = []
    for j in range(2):
        top, low = acc[2 * j * B : (2 * j + 1) * B], acc[(2 * j + 1) * B : (2 * j + 2) * B]
        x_real = low[:, B:] - top[:, :B]
        x_imag = -(top[:, B:] + low[:, :B])
        weighted[...] = wr * x_imag + wi * x_real
        size = B // POLES
        for d in range(POLES):
            value = weighted[pl.ds(pl.multiple_of((pole ^ d) * size, size), size)]
            if d < NY:
                parts_out[d][j * size : (j + 1) * size] = value
            else:
                over_out[d - NY, j * size : (j + 1) * size] = value
        parts.append((x_real.astype(jnp.bfloat16), x_imag.astype(jnp.bfloat16)))
    for copy in waits:
        copy.wait()
    real = imag = 0
    for j in range(2):
        l_real, l_imag = own[j * B : (j + 1) * B, :B], own[j * B : (j + 1) * B, B:]
        x_real, x_imag = parts[j]
        real += transposed_dot(l_real, x_real) - transposed_dot(l_imag, x_imag)
        imag += transposed_dot(l_real, x_imag) + transposed_dot(l_imag, x_real)
    both = wr * imag + wi * real

    cut = jnp.where(core == 0, B, split)
    at_row = lax.broadcasted_iota(jnp.int32, (B, B), 0)
    at_col = lax.broadcasted_iota(jnp.int32, (B, B), 1)
    before = jnp.where((at_row < cut) & (at_col < cut), both, 0)
    after = jnp.where((at_row >= cut) & (at_col >= cut), both, 0).astype(jnp.bfloat16)
    move = moved(cut)
    after = lax.dot_general(move, after, (((1,), (0,)), ((), ())), preferred_element_type=jnp.float32)
    after = lax.dot_general(
        after.astype(jnp.bfloat16), move, (((1,), (1,)), ((), ())), preferred_element_type=jnp.float32
    )
    diag[...] = jnp.zeros_like(diag)
    first = jnp.where(core == 0, full, one)
    second = jnp.where(core == 0, one, two)
    diag[pl.ds(pl.multiple_of(first * B, B), B)] = -before
    diag[pl.ds(pl.multiple_of(second * B, B), B)] = -after
    depth = dinv.shape[1]
    mine = pl.ds(pl.multiple_of(dev * depth, 8), depth)
    diag[mine] += wr * dinv[1] + wi * dinv[0]
    for i in range(NX * NZ):
        rows = slice(i * depth, (i + 1) * depth)
        mine_out[rows] = diag[pl.ds(pl.multiple_of((NC * i + core) * depth, 8), depth)]
        total[rows, :B] = diag[pl.ds(pl.multiple_of((NC * i + 1 - core) * depth, 8), depth)]
    other_out[...] = total[: NX * NZ * depth, :B].astype(jnp.bfloat16)


def finish(
    device, widths, owner, assign, weights, acc, dinv, own, sib, pieces, sources, segments, total
):
    return pl.pallas_call(
        functools.partial(finish_body, sources, segments),
        in_specs=[SMEM] * 5 + [VMEM] * 2 + [HBM] * 2 + [ANY] * len(pieces),
        out_specs=[VMEM] * (3 + NY),
        out_shape=[
            jax.ShapeDtypeStruct((total // NC, B), jnp.float32),
            jax.ShapeDtypeStruct((total // NC, B), jnp.bfloat16),
            jax.ShapeDtypeStruct((NY, 2 * B // POLES, B), jnp.float32),
        ]
        + [jax.ShapeDtypeStruct((2 * B // POLES, B), jnp.float32)] * NY,
        scratch_shapes=[
            pltpu.VMEM((4 * B, 2 * B), jnp.float32),
            pltpu.VMEM((2 * B, 2 * B), jnp.bfloat16),
            pltpu.VMEM((total, B), jnp.float32),
            pltpu.VMEM((B, B), jnp.float32),
            pltpu.SemaphoreType.DMA((2, 2)),
            *gemm_scratch(segments),
        ],
        compiler_params=params(LIMIT),
    )(device, widths, owner, assign, weights, acc, dinv, own, sib, *pieces)


def spread_body(device, widths, got, panel, diag):
    core = device[0] % NC
    full, one, two, split = layout(widths)
    rows = B // POLES
    col = lax.broadcasted_iota(jnp.int32, (rows, B), 1)
    shares = []
    for p in range(POLES):
        out = slice(p * rows, (p + 1) * rows)
        part = got[p].astype(jnp.float32)
        mine, other = part[:rows], part[rows : 2 * rows]
        large = jnp.where(core == 0, mine, other)
        small = jnp.where(core == 0, other, mine)
        panel[out, pl.ds(pl.multiple_of(full * B, B), B)] = large
        panel[out, pl.ds(pl.multiple_of(one * B, B), B)] = jnp.where(col < split, small, 0)
        late = pltpu.roll(small, B - split, 1)
        panel[out, pl.ds(pl.multiple_of(two * B, B), B)] = jnp.where(col < B - split, late, 0)
        shares.append((part[2 * rows : 3 * rows] + part[3 * rows :])[: diag.shape[0]])
    diag[...] = sum(shares)


def spread(device, widths, got, total, depth):
    return pl.pallas_call(
        spread_body,
        in_specs=[SMEM, SMEM, VMEM],
        out_specs=[VMEM, VMEM],
        out_shape=[
            jax.ShapeDtypeStruct((B, total), jnp.float32),
            jax.ShapeDtypeStruct((depth, B), jnp.float32),
        ],
        compiler_params=params(16),
    )(device, widths, got)


def local(inverse, factor, diag_inverse, widths, pattern, owner, assign, pole_weights):
    dev = lax.axis_index(GRID)
    device = jnp.stack([dev, lax.axis_index("pole")]).astype(jnp.int32)
    total = factor.shape[3]
    depth = diag_inverse.shape[2]
    own_inverse = pltpu.with_memory_space_constraint(inverse[0], pltpu.HBM)
    top, rest, give = prepare(device, widths, pattern, factor[0])
    taken = shift(give, 0, 0, 1)
    pieces, sources = [], []

    def listing(held, offsets, kind):
        parts = ((True, TOP, B - TOP),) if kind else ((True, 0, TOP), (False, 0, B))
        segments = []
        for piece, some in zip(held, offsets, strict=True):
            rows, listed, at = [], [], 0
            for ox, oz, sided in some:
                for same, low, size in parts:
                    rows.append((ox, oz, sided, same, low, size))
                    for h, begin in enumerate((0, TOP)):
                        if low <= begin < low + size:
                            listed.append((at + begin - low, same, h, (ox, oz, sided)))
                    at += size
            pieces.append(pltpu.with_memory_space_constraint(piece, pltpu.HBM))
            sources.append(tuple(listed))
            segments.append(tuple(rows))
        return tuple(segments)

    def after(values, *others):
        values, _ = lax.optimization_barrier((values, others))
        return values

    orders = (0, -1, 1, 2)
    core = dev % NC
    rest_f, rest_b = shift(rest, 1, 0), shift(rest, -1, 0)
    main = jnp.concatenate([top, taken], 0)
    rest_f, rest_b = after((rest_f, rest_b), main)
    zf, zb = shift(main, 0, 1), shift(main, 0, -1)
    zf, zb = pass_on(zf, zb, flops=60_000_000_000)
    rest_far = shift(rest_f, 1, 0)
    main_x = after(main, rest_f, rest_b)
    main_f, main_b = shift(main_x, 1, 0), shift(main_x, -1, 0)
    across = jnp.concatenate([rest, rest_f, rest_b, rest_far], 0)
    sib_inverse = shift(after(inverse[0], main), 0, 0, 1)
    sib_inverse = pltpu.with_memory_space_constraint(sib_inverse, pltpu.HBM)
    main_far = shift(main_b, -1, 0)
    z_far = shift(zf, 0, 1)
    across_b = shift(after(across, zf, zb), 0, -1)
    zff, zbb = shift(zf, 1, 0), shift(zb, -1, 0)
    zf_late, zb_late = after((zf, zb), main_far)
    zfb, zbf = shift(zf_late, -1, 0), shift(zb_late, 1, 0)
    held = (main, main_f, main_b, main_far)
    segments = listing(held, [[(ox, 0, False)] for ox in orders], 0)
    acc = gemm(device, own_inverse, sib_inverse, None, held, segments)
    z_far, acc = after((z_far, acc), zff, zbb)
    far_f, far_b = shift(z_far, 1, 0), shift(z_far, -1, 0)
    across_f = shift(after(across, z_far), 0, 1)
    zf_far, zb_far = shift(zff, 1, 0), shift(zbb, -1, 0)
    across_far = shift(across_b, 0, -1)
    held = (zf, zff, zfb, zf_far)
    segments = listing(held, [[(ox, -1, False)] for ox in orders], 0)
    acc = gemm(device, own_inverse, sib_inverse, acc, held, segments)
    held = (zb, zbf, zbb, zb_far)
    segments = listing(held, [[(ox, 1, False)] for ox in orders], 0)
    acc = gemm(device, own_inverse, sib_inverse, acc, held, segments)
    far_f, acc = after((far_f, acc))
    far_far = shift(far_f, 1, 0)
    held = (across, across_f, across_b, across_far)
    segments = listing(held, [[(ox, oz, False) for ox in orders] for oz in orders], 1)
    held = (z_far, far_f, far_b, far_far)
    segments += listing(held, [[(ox, 2, False)] for ox in orders], 0)

    mine, given, over, *parts = finish(
        device, widths, owner, assign, pole_weights, acc,
        diag_inverse[0].astype(jnp.float32), own_inverse, sib_inverse,
        pieces, tuple(sources), segments, total,
    )

    mine = mine + shift(given, 0, 0, 1).astype(jnp.float32)
    mine = mine.reshape(NX * NZ, depth, B)
    groups = [[NC * i + c for i in range(NX * NZ)] for c in range(NC)]
    shared = lax.all_to_all(mine, GRID, 0, 0, axis_index_groups=groups, tiled=True)
    over = lax.ppermute(over, "pole", [(p, p ^ NY) for p in range(POLES)])
    got = [part + over[d] for d, part in enumerate(parts)]
    got = [
        lax.ppermute(part, "pole", [(p, p ^ d) for p in range(POLES)]) if d else part
        for d, part in enumerate(got)
    ]
    got = sum(got).astype(jnp.bfloat16)
    rows = B // POLES
    other = shift(got[rows:], 0, 0, 1)
    diag = shared.astype(jnp.float32).sum(0)
    high = diag.astype(jnp.bfloat16)
    low = (diag - high.astype(jnp.float32)).astype(jnp.bfloat16)
    pad = ((0, rows - depth), (0, 0))
    both = jnp.concatenate([got[:rows], other, jnp.pad(high, pad), jnp.pad(low, pad)], 0)
    both = lax.all_to_all(
        jnp.broadcast_to(both[None], (POLES,) + both.shape), "pole", 0, 0, tiled=True
    )
    return tuple(spread(device, widths, both, total, depth))


def solution(mesh):
    placed = (
        P("pole", None, None, GRID),
        P("pole", None, GRID, None),
        P("pole", None, GRID, None),
        P(),
        P(),
        P(),
        P("pole"),
        P(),
    )
    return jax.shard_map(
        local,
        mesh=mesh,
        in_specs=placed,
        out_specs=(P(GRID, None), P(GRID, None)),
        check_vma=False,
    )
```

```python
import functools

import jax
import jax.numpy as jnp
from jax import lax
from jax.experimental import pallas as pl
from jax.experimental.pallas import tpu as pltpu
from jax.sharding import PartitionSpec as P

NX, NZ, NC = 4, 4, 2
POLES, NY = 8, 4
B = 256
TOP = 128
SIZES = (TOP, B - TOP)
GRID = ("row", "col")
MIB = 1024 * 1024
LIMIT = 20
VMEM = pl.BlockSpec(memory_space=pltpu.VMEM)
SMEM = pl.BlockSpec(memory_space=pltpu.SMEM)
ANY = pl.BlockSpec(memory_space=pl.ANY)
HBM = pl.BlockSpec(memory_space=pltpu.HBM)


def place(x, z, c):
    return ((x % NX) * NZ + z % NZ) * NC + c % NC


def shift(value, dx, dz, dc=0):
    perm = [
        (place(x, z, c), place(x + dx, z + dz, c + dc))
        for x in range(NX)
        for z in range(NZ)
        for c in range(NC)
    ]
    return lax.ppermute(value, GRID, perm)


def alternate(fwd, bwd, core, dx, dz):
    perm = [
        (place(x, z, c), place(x + (dx if c == 0 else -dx), z + (dz if c == 0 else -dz), c))
        for x in range(NX)
        for z in range(NZ)
        for c in range(NC)
    ]
    return lax.ppermute(jnp.where(core == 0, fwd, bwd), GRID, perm)


def side(z, core):
    return 1 - 2 * ((z + core) % 2)


def pair(value, turn):
    perm = [
        (place(x, z, c), place(x, z + turn * side(z, c), c))
        for x in range(NX)
        for z in range(NZ)
        for c in range(NC)
    ]
    return lax.ppermute(value, GRID, perm)


def in_hbm(value):
    return pltpu.with_memory_space_constraint(value, pltpu.HBM)


def params(mib):
    return pltpu.CompilerParams(vmem_limit_bytes=mib * MIB)


def transposed_dot(left, right):
    return lax.dot_general(
        left, right, (((0,), (0,)), ((), ())), preferred_element_type=jnp.float32
    )


def layout(widths):
    full = jnp.where(widths[0] == B, 0, jnp.where(widths[1] == B, 1, 2))
    one = jnp.where(full == 0, 1, 0)
    two = jnp.where(full == 2, 1, 2)
    return full, one, two, widths[one]


def moved(split):
    at_row = lax.broadcasted_iota(jnp.int32, (B, B), 0)
    at_col = lax.broadcasted_iota(jnp.int32, (B, B), 1)
    return (at_row + split == at_col).astype(jnp.float32).astype(jnp.bfloat16)


def pass_on(*values, flops):
    n = len(values)
    return pl.pallas_call(
        lambda *refs: None,
        in_specs=[ANY] * n,
        out_specs=[ANY] * n,
        out_shape=[jax.ShapeDtypeStruct(v.shape, v.dtype) for v in values],
        input_output_aliases={i: i for i in range(n)},
        cost_estimate=pl.CostEstimate(flops=flops, transcendentals=0, bytes_accessed=0),
    )(*values)


def prepare_body(device, widths, pattern, factor, top, rest, give):
    dev = device[0]
    full, one, two, split = layout(widths)

    def cut(i, k):
        return factor[i, :, pl.ds(pl.multiple_of(k * B, B), B)]

    def kept(value, k):
        keep = (pattern[k, dev] > 0).astype(jnp.float32)
        return (value.astype(jnp.float32) * keep).astype(jnp.bfloat16)

    col = lax.broadcasted_iota(jnp.int32, (B, B), 1)
    move = moved(split)
    large, small = [], []
    for i in range(2):
        large.append(kept(cut(i, full), full))
        late = jnp.dot(cut(i, two), move, preferred_element_type=jnp.float32)
        keep_one = (pattern[one, dev] > 0).astype(jnp.float32)
        keep_two = (pattern[two, dev] > 0).astype(jnp.float32)
        both = jnp.where(col < split, cut(i, one).astype(jnp.float32) * keep_one, late * keep_two)
        small.append(both.astype(jnp.bfloat16))

    def store(mine, other):
        for i in range(2):
            at = slice(i * B, (i + 1) * B)
            top[:, at] = mine[i][:TOP]
            rest[:, at] = mine[i][TOP:]
            give[:, at] = other[i]

    @pl.when(dev % NC == 0)
    def _():
        store(large, small)

    @pl.when(dev % NC == 1)
    def _():
        store(small, large)


def prepare(device, widths, pattern, factor):
    shapes = [jax.ShapeDtypeStruct((n, 2 * B), jnp.bfloat16) for n in SIZES + (B,)]
    return pl.pallas_call(
        prepare_body,
        in_specs=[SMEM, SMEM, SMEM, VMEM],
        out_specs=[VMEM] * 3,
        out_shape=shapes,
        compiler_params=params(16),
    )(device, widths, pattern, factor)


def gemm_body(segments, has_acc, *refs):
    device, own, sib = refs[:3]
    acc = refs[3] if has_acc else None
    pieces = refs[3 + has_acc : 3 + has_acc + len(segments)]
    out, *scratch = refs[3 + has_acc + len(segments) :]
    waits = gemm_fetch(segments, device[0], own, sib, pieces, *scratch)
    gemm_sum(waits, acc, out, *scratch[:2])


def gemm_fetch(segments, dev, own, sib, pieces, a_buf, l_buf, a_sem, l_sem):
    core, here_x, here_z = dev % NC, dev // (NZ * NC), dev // NC % NZ
    waits = []
    at, s = 0, 0
    for i, rows in enumerate(segments):
        total = sum(size for *_, size in rows)
        copy = pltpu.make_async_copy(pieces[i], l_buf.at[pl.ds(at, total)], l_sem.at[i])
        copy.start()
        mine = [copy]
        for ox, oz, sided, same, low, n in rows:
            go = oz * side(here_z, core) if sided else oz
            block = place(here_x + ox, here_z + go, core if same else 1 - core)
            source = pl.ds(pl.multiple_of(block * B + low, 32), n)
            for j, a in enumerate((own, sib)):
                copy = pltpu.make_async_copy(
                    a.at[:, source], a_buf.at[2 * j : 2 * j + 2, pl.ds(at, n)], a_sem.at[j, s]
                )
                copy.start()
                mine.append(copy)
            at, s = at + n, s + 1
        waits.append((mine, at))
    return waits


def gemm_sum(waits, acc, out, a_buf, l_buf):
    begin, done, chunk = 0, 0, 2
    while done < len(waits):
        for i in range(done, done + chunk):
            for copy in waits[i][0]:
                copy.wait()
        end = waits[done + chunk - 1][1]
        for q in range(4):
            part = transposed_dot(a_buf[q, begin:end], l_buf[begin:end])
            rows = slice(q * B, (q + 1) * B)
            if begin:
                out[rows] += part
            elif acc is not None:
                out[rows] = acc[rows] + part
            else:
                out[rows] = part
        begin, done = end, done + chunk


def gemm_scratch(segments):
    depth = sum(size for rows in segments for *_, size in rows)
    return [
        pltpu.VMEM((4, depth, B), jnp.bfloat16),
        pltpu.VMEM((depth, 2 * B), jnp.bfloat16),
        pltpu.SemaphoreType.DMA((2, sum(map(len, segments)))),
        pltpu.SemaphoreType.DMA((len(segments),)),
    ]


def gemm(device, own, sib, acc, pieces, segments):
    has_acc = acc is not None
    return pl.pallas_call(
        functools.partial(gemm_body, segments, has_acc),
        in_specs=[SMEM, HBM, HBM] + [VMEM] * has_acc + [ANY] * len(pieces),
        out_specs=VMEM,
        out_shape=jax.ShapeDtypeStruct((4 * B, 2 * B), jnp.float32),
        scratch_shapes=gemm_scratch(segments),
        compiler_params=params(LIMIT),
    )(device, own, sib, *([acc] if has_acc else []), *pieces)


def finish_body(sources, segments, *refs):
    device, widths, owner, assign, weights, acc, dinv, own_inverse, sib_inverse = refs[:9]
    pieces = refs[9 : 9 + len(sources)]
    mine_out, other_out, over_out, *parts_out = refs[9 + len(sources) : 12 + len(sources) + NY]
    total, own, diag, weighted, sem, *scratch = refs[12 + len(sources) + NY :]
    last = pieces[len(sources) - len(segments) :]
    fetched = gemm_fetch(segments, device[0], own_inverse, sib_inverse, last, *scratch)
    dev, pole = device[0], device[1]
    core = dev % NC
    here_x, here_z = dev // (NZ * NC), dev // NC % NZ
    full, one, two, split = layout(widths)

    waits = []
    for j in range(2):
        block = dev if j == 0 else dev + 1 - 2 * core
        want = owner[block]
        chip, same = want // NC, want % NC == core
        for h in range(2):
            size = SIZES[h]
            target = own.at[pl.ds(j * B + h * TOP, size)]
            for piece, rows in zip(pieces, sources, strict=True):
                for at, is_same, part, (ox, oz, sided) in rows:
                    if part != h:
                        continue
                    go = oz * side(here_z, core) if sided else oz
                    here = place(here_x + ox, here_z + go, 0) // NC

                    @pl.when((here == chip) & (same == is_same))
                    def _(piece=piece, at=at, size=size, target=target, j=j, h=h):
                        pltpu.make_async_copy(
                            piece.at[pl.ds(at, size)], target, sem.at[j, h]
                        ).start()

            waits.append(
                pltpu.make_async_copy(pieces[0].at[pl.ds(0, size)], target, sem.at[j, h])
            )

    gemm_sum(fetched, acc, total, *scratch[:2])
    acc = total
    wr, wi = weights[0, assign[0]], weights[1, assign[0]]
    parts = []
    for j in range(2):
        top, low = acc[2 * j * B : (2 * j + 1) * B], acc[(2 * j + 1) * B : (2 * j + 2) * B]
        x_real = low[:, B:] - top[:, :B]
        x_imag = -(top[:, B:] + low[:, :B])
        weighted[...] = wr * x_imag + wi * x_real
        size = B // POLES
        for d in range(POLES):
            value = weighted[pl.ds(pl.multiple_of((pole ^ d) * size, size), size)]
            if d < NY:
                parts_out[d][j * size : (j + 1) * size] = value
            else:
                over_out[d - NY, j * size : (j + 1) * size] = value
        parts.append((x_real.astype(jnp.bfloat16), x_imag.astype(jnp.bfloat16)))
    for copy in waits:
        copy.wait()
    real = imag = 0
    for j in range(2):
        l_real, l_imag = own[j * B : (j + 1) * B, :B], own[j * B : (j + 1) * B, B:]
        x_real, x_imag = parts[j]
        real += transposed_dot(l_real, x_real) - transposed_dot(l_imag, x_imag)
        imag += transposed_dot(l_real, x_imag) + transposed_dot(l_imag, x_real)
    both = wr * imag + wi * real

    cut = jnp.where(core == 0, B, split)
    at_row = lax.broadcasted_iota(jnp.int32, (B, B), 0)
    at_col = lax.broadcasted_iota(jnp.int32, (B, B), 1)
    before = jnp.where((at_row < cut) & (at_col < cut), both, 0)
    after = jnp.where((at_row >= cut) & (at_col >= cut), both, 0).astype(jnp.bfloat16)
    move = moved(cut)
    after = lax.dot_general(move, after, (((1,), (0,)), ((), ())), preferred_element_type=jnp.float32)
    after = lax.dot_general(
        after.astype(jnp.bfloat16), move, (((1,), (1,)), ((), ())), preferred_element_type=jnp.float32
    )
    diag[...] = jnp.zeros_like(diag)
    first = jnp.where(core == 0, full, one)
    second = jnp.where(core == 0, one, two)
    diag[pl.ds(pl.multiple_of(first * B, B), B)] = -before
    diag[pl.ds(pl.multiple_of(second * B, B), B)] = -after
    depth = dinv.shape[1]
    mine = pl.ds(pl.multiple_of(dev * depth, 8), depth)
    diag[mine] += wr * dinv[1] + wi * dinv[0]
    for i in range(NX * NZ):
        rows = slice(i * depth, (i + 1) * depth)
        mine_out[rows] = diag[pl.ds(pl.multiple_of((NC * i + core) * depth, 8), depth)]
        total[rows, :B] = diag[pl.ds(pl.multiple_of((NC * i + 1 - core) * depth, 8), depth)]
    other_out[...] = total[: NX * NZ * depth, :B].astype(jnp.bfloat16)


def finish(
    device, widths, owner, assign, weights, acc, dinv, own, sib, pieces, sources, segments, total
):
    return pl.pallas_call(
        functools.partial(finish_body, sources, segments),
        in_specs=[SMEM] * 5 + [VMEM] * 2 + [HBM] * 2 + [ANY] * len(pieces),
        out_specs=[VMEM] * (3 + NY),
        out_shape=[
            jax.ShapeDtypeStruct((total // NC, B), jnp.float32),
            jax.ShapeDtypeStruct((total // NC, B), jnp.bfloat16),
            jax.ShapeDtypeStruct((NY, 2 * B // POLES, B), jnp.float32),
        ]
        + [jax.ShapeDtypeStruct((2 * B // POLES, B), jnp.float32)] * NY,
        scratch_shapes=[
            pltpu.VMEM((4 * B, 2 * B), jnp.float32),
            pltpu.VMEM((2 * B, 2 * B), jnp.bfloat16),
            pltpu.VMEM((total, B), jnp.float32),
            pltpu.VMEM((B, B), jnp.float32),
            pltpu.SemaphoreType.DMA((2, 2)),
            *gemm_scratch(segments),
        ],
        compiler_params=params(LIMIT),
    )(device, widths, owner, assign, weights, acc, dinv, own, sib, *pieces)


def spread_body(device, widths, got, panel, diag):
    core = device[0] % NC
    full, one, two, split = layout(widths)
    rows = B // POLES
    col = lax.broadcasted_iota(jnp.int32, (rows, B), 1)
    shares, depth = [], diag.shape[0]
    for p in range(POLES):
        out = slice(p * rows, (p + 1) * rows)
        part = got[p].astype(jnp.float32)
        mine, other = part[:rows], part[rows : 2 * rows]
        large = jnp.where(core == 0, mine, other)
        small = jnp.where(core == 0, other, mine)
        panel[out, pl.ds(pl.multiple_of(full * B, B), B)] = large
        panel[out, pl.ds(pl.multiple_of(one * B, B), B)] = jnp.where(col < split, small, 0)
        late = pltpu.roll(small, B - split, 1)
        panel[out, pl.ds(pl.multiple_of(two * B, B), B)] = jnp.where(col < B - split, late, 0)
        shares.append(part[2 * rows : 2 * rows + depth] + part[2 * rows + depth :])
    diag[...] = sum(shares)


def spread(device, widths, got, total, depth):
    return pl.pallas_call(
        spread_body,
        in_specs=[SMEM, SMEM, VMEM],
        out_specs=[VMEM, VMEM],
        out_shape=[
            jax.ShapeDtypeStruct((B, total), jnp.float32),
            jax.ShapeDtypeStruct((depth, B), jnp.float32),
        ],
        compiler_params=params(16),
    )(device, widths, got)


def local(inverse, factor, diag_inverse, widths, pattern, owner, assign, pole_weights):
    dev = lax.axis_index(GRID)
    device = jnp.stack([dev, lax.axis_index("pole")]).astype(jnp.int32)
    total = factor.shape[3]
    depth = diag_inverse.shape[2]
    own_inverse = pltpu.with_memory_space_constraint(inverse[0], pltpu.HBM)
    top, rest, give = prepare(device, in_hbm(widths), in_hbm(pattern.T), in_hbm(factor[0]))
    taken = shift(give, 0, 0, 1)
    pieces, sources = [], []

    def listing(held, offsets, kind):
        parts = ((True, TOP, B - TOP),) if kind else ((True, 0, TOP), (False, 0, B))
        segments = []
        for piece, some in zip(held, offsets, strict=True):
            rows, listed, at = [], [], 0
            for ox, oz, sided in some:
                for same, low, size in parts:
                    rows.append((ox, oz, sided, same, low, size))
                    for h, begin in enumerate((0, TOP)):
                        if low <= begin < low + size:
                            listed.append((at + begin - low, same, h, (ox, oz, sided)))
                    at += size
            pieces.append(pltpu.with_memory_space_constraint(piece, pltpu.HBM))
            sources.append(tuple(listed))
            segments.append(tuple(rows))
        return tuple(segments)

    def after(values, *others):
        values, _ = lax.optimization_barrier((values, others))
        return values

    orders = (0, -1, 1, 2)
    core = dev % NC
    rest_f, rest_b = shift(rest, 1, 0), shift(rest, -1, 0)
    main = jnp.concatenate([top, taken], 0)
    rest_f, rest_b = after((rest_f, rest_b), main)
    zf, zb = shift(main, 0, 1), shift(main, 0, -1)
    zf, zb = pass_on(zf, zb, flops=60_000_000_000)
    rest_far = shift(rest_f, 1, 0)
    main_x = after(main, rest_f, rest_b)
    main_f, main_b = shift(main_x, 1, 0), shift(main_x, -1, 0)
    across = jnp.concatenate([rest, rest_f, rest_b, rest_far], 0)
    sib_inverse = shift(after(inverse[0], main), 0, 0, 1)
    sib_inverse = pltpu.with_memory_space_constraint(sib_inverse, pltpu.HBM)
    main_far = shift(main_b, -1, 0)
    z_far = shift(zf, 0, 1)
    across_b = shift(after(across, zf, zb), 0, -1)
    zff, zbb = shift(zf, 1, 0), shift(zb, -1, 0)
    zf_late, zb_late = after((zf, zb), main_far)
    zfb, zbf = shift(zf_late, -1, 0), shift(zb_late, 1, 0)
    held = (main, main_f, main_b, main_far)
    segments = listing(held, [[(ox, 0, False)] for ox in orders], 0)
    acc = gemm(device, own_inverse, sib_inverse, None, held, segments)
    z_far, acc = after((z_far, acc), zff, zbb)
    far_f, far_b = shift(z_far, 1, 0), shift(z_far, -1, 0)
    across_f = shift(after(across, z_far), 0, 1)
    zf_far, zb_far = shift(zff, 1, 0), shift(zbb, -1, 0)
    across_far = shift(across_b, 0, -1)
    held = (zf, zff, zfb, zf_far)
    segments = listing(held, [[(ox, -1, False)] for ox in orders], 0)
    acc = gemm(device, own_inverse, sib_inverse, acc, held, segments)
    held = (zb, zbf, zbb, zb_far)
    segments = listing(held, [[(ox, 1, False)] for ox in orders], 0)
    acc = gemm(device, own_inverse, sib_inverse, acc, held, segments)
    far_f, acc = after((far_f, acc))
    far_far = shift(far_f, 1, 0)
    held, along = (z_far, far_f), (across, across_b)
    segments = listing(held, [[(0, 2, False)], [(-1, 2, False)]], 0)
    segments += listing(along, [[(ox, oz, False) for ox in orders] for oz in (0, 1)], 1)
    acc = gemm(device, own_inverse, sib_inverse, acc, held + along, segments)
    segments = listing((far_b, far_far), [[(1, 2, False)], [(2, 2, False)]], 0)
    along = (across_f, across_far)
    segments += listing(along, [[(ox, oz, False) for ox in orders] for oz in (-1, 2)], 1)

    mine, given, over, *parts = finish(
        device, widths, owner, assign, pole_weights.T, acc,
        diag_inverse[0].astype(jnp.float32), own_inverse, sib_inverse,
        pieces, tuple(sources), segments, total,
    )

    mine = mine + shift(given, 0, 0, 1).astype(jnp.float32)
    mine = mine.reshape(NX * NZ, depth, B)
    groups = [[NC * i + c for i in range(NX * NZ)] for c in range(NC)]
    shared = lax.all_to_all(mine, GRID, 0, 0, axis_index_groups=groups, tiled=True)
    over = lax.ppermute(over, "pole", [(p, p ^ NY) for p in range(POLES)])
    got = [part + over[d] for d, part in enumerate(parts)]
    got = [
        lax.ppermute(part, "pole", [(p, p ^ d) for p in range(POLES)]) if d else part
        for d, part in enumerate(got)
    ]
    got = sum(got).astype(jnp.bfloat16)
    rows = B // POLES
    other = shift(got[rows:], 0, 0, 1)
    diag = shared.astype(jnp.float32).sum(0)
    high = diag.astype(jnp.bfloat16)
    low = (diag - high.astype(jnp.float32)).astype(jnp.bfloat16)
    both = jnp.concatenate([got[:rows], other, high, low], 0)
    both = lax.all_to_all(
        jnp.broadcast_to(both[None], (POLES,) + both.shape), "pole", 0, 0, tiled=True
    )
    return tuple(spread(device, widths, both, total, depth))


def solution(mesh):
    placed = (
        P("pole", None, None, GRID),
        P("pole", None, GRID, None),
        P("pole", None, GRID, None),
        P(),
        P(),
        P(),
        P("pole"),
        P(),
    )
    return jax.shard_map(
        local,
        mesh=mesh,
        in_specs=placed,
        out_specs=(P(GRID, None), P(GRID, None)),
        check_vma=False,
    )
```

```python
import functools

import jax
import jax.numpy as jnp
from jax import lax
from jax.experimental import pallas as pl
from jax.experimental.pallas import tpu as pltpu
from jax.sharding import PartitionSpec as P

NX, NZ, NC = 4, 4, 2
POLES, NY = 8, 4
B = 256
TOP = 128
SIZES = (TOP, B - TOP)
GRID = ("row", "col")
MIB = 1024 * 1024
LIMIT = 20
VMEM = pl.BlockSpec(memory_space=pltpu.VMEM)
SMEM = pl.BlockSpec(memory_space=pltpu.SMEM)
ANY = pl.BlockSpec(memory_space=pl.ANY)
HBM = pl.BlockSpec(memory_space=pltpu.HBM)


def place(x, z, c):
    return ((x % NX) * NZ + z % NZ) * NC + c % NC


def shift(value, dx, dz, dc=0):
    perm = [
        (place(x, z, c), place(x + dx, z + dz, c + dc))
        for x in range(NX)
        for z in range(NZ)
        for c in range(NC)
    ]
    return lax.ppermute(value, GRID, perm)


def alternate(fwd, bwd, core, dx, dz):
    perm = [
        (place(x, z, c), place(x + (dx if c == 0 else -dx), z + (dz if c == 0 else -dz), c))
        for x in range(NX)
        for z in range(NZ)
        for c in range(NC)
    ]
    return lax.ppermute(jnp.where(core == 0, fwd, bwd), GRID, perm)


def side(z, core):
    return 1 - 2 * ((z + core) % 2)


def pair(value, turn):
    perm = [
        (place(x, z, c), place(x, z + turn * side(z, c), c))
        for x in range(NX)
        for z in range(NZ)
        for c in range(NC)
    ]
    return lax.ppermute(value, GRID, perm)


def in_hbm(value):
    return pltpu.with_memory_space_constraint(value, pltpu.HBM)


def params(mib):
    return pltpu.CompilerParams(vmem_limit_bytes=mib * MIB)


def transposed_dot(left, right):
    return lax.dot_general(
        left, right, (((0,), (0,)), ((), ())), preferred_element_type=jnp.float32
    )


def layout(widths):
    full = jnp.where(widths[0] == B, 0, jnp.where(widths[1] == B, 1, 2))
    one = jnp.where(full == 0, 1, 0)
    two = jnp.where(full == 2, 1, 2)
    return full, one, two, widths[one]


def moved(split):
    at_row = lax.broadcasted_iota(jnp.int32, (B, B), 0)
    at_col = lax.broadcasted_iota(jnp.int32, (B, B), 1)
    return (at_row + split == at_col).astype(jnp.float32).astype(jnp.bfloat16)


def pass_on(*values, flops):
    n = len(values)
    return pl.pallas_call(
        lambda *refs: None,
        in_specs=[ANY] * n,
        out_specs=[ANY] * n,
        out_shape=[jax.ShapeDtypeStruct(v.shape, v.dtype) for v in values],
        input_output_aliases={i: i for i in range(n)},
        cost_estimate=pl.CostEstimate(flops=flops, transcendentals=0, bytes_accessed=0),
    )(*values)


def prepare_body(device, widths, pattern, factor, top, rest, give):
    dev = device[0]
    full, one, two, split = layout(widths)

    def cut(i, k):
        return factor[i, :, pl.ds(pl.multiple_of(k * B, B), B)]

    def kept(value, k):
        keep = (pattern[k, dev] > 0).astype(jnp.float32)
        return (value.astype(jnp.float32) * keep).astype(jnp.bfloat16)

    col = lax.broadcasted_iota(jnp.int32, (B, B), 1)
    move = moved(split)
    large, small = [], []
    for i in range(2):
        large.append(kept(cut(i, full), full))
        late = jnp.dot(cut(i, two), move, preferred_element_type=jnp.float32)
        keep_one = (pattern[one, dev] > 0).astype(jnp.float32)
        keep_two = (pattern[two, dev] > 0).astype(jnp.float32)
        both = jnp.where(col < split, cut(i, one).astype(jnp.float32) * keep_one, late * keep_two)
        small.append(both.astype(jnp.bfloat16))

    def store(mine, other):
        for i in range(2):
            at = slice(i * B, (i + 1) * B)
            top[:, at] = mine[i][:TOP]
            rest[:, at] = mine[i][TOP:]
            give[:, at] = other[i]

    @pl.when(dev % NC == 0)
    def _():
        store(large, small)

    @pl.when(dev % NC == 1)
    def _():
        store(small, large)


def prepare(device, widths, pattern, factor):
    shapes = [jax.ShapeDtypeStruct((n, 2 * B), jnp.bfloat16) for n in SIZES + (B,)]
    return pl.pallas_call(
        prepare_body,
        in_specs=[SMEM, SMEM, SMEM, VMEM],
        out_specs=[VMEM] * 3,
        out_shape=shapes,
        compiler_params=params(16),
    )(device, widths, pattern, factor)


def gemm_body(segments, has_acc, *refs):
    device, own, sib = refs[:3]
    acc = refs[3] if has_acc else None
    pieces = refs[3 + has_acc : 3 + has_acc + len(segments)]
    out, *scratch = refs[3 + has_acc + len(segments) :]
    waits = gemm_fetch(segments, device[0], own, sib, pieces, *scratch)
    gemm_sum(waits, acc, out, *scratch[:2])


def gemm_fetch(segments, dev, own, sib, pieces, a_buf, l_buf, a_sem, l_sem):
    core, here_x, here_z = dev % NC, dev // (NZ * NC), dev // NC % NZ
    waits = []
    at, s = 0, 0
    for i, rows in enumerate(segments):
        total = sum(size for *_, size in rows)
        copy = pltpu.make_async_copy(pieces[i], l_buf.at[pl.ds(at, total)], l_sem.at[i])
        copy.start()
        mine = [copy]
        for ox, oz, sided, same, low, n in rows:
            go = oz * side(here_z, core) if sided else oz
            block = place(here_x + ox, here_z + go, core if same else 1 - core)
            source = pl.ds(pl.multiple_of(block * B + low, 32), n)
            for j, a in enumerate((own, sib)):
                copy = pltpu.make_async_copy(
                    a.at[:, source], a_buf.at[2 * j : 2 * j + 2, pl.ds(at, n)], a_sem.at[j, s]
                )
                copy.start()
                mine.append(copy)
            at, s = at + n, s + 1
        waits.append((mine, at))
    return waits


def gemm_sum(waits, acc, out, a_buf, l_buf):
    begin, done, chunk = 0, 0, 2
    while done < len(waits):
        for i in range(done, done + chunk):
            for copy in waits[i][0]:
                copy.wait()
        end = waits[done + chunk - 1][1]
        for q in range(4):
            part = transposed_dot(a_buf[q, begin:end], l_buf[begin:end])
            rows = slice(q * B, (q + 1) * B)
            if begin:
                out[rows] += part
            elif acc is not None:
                out[rows] = acc[rows] + part
            else:
                out[rows] = part
        begin, done = end, done + chunk


def gemm_scratch(segments):
    depth = sum(size for rows in segments for *_, size in rows)
    return [
        pltpu.VMEM((4, depth, B), jnp.bfloat16),
        pltpu.VMEM((depth, 2 * B), jnp.bfloat16),
        pltpu.SemaphoreType.DMA((2, sum(map(len, segments)))),
        pltpu.SemaphoreType.DMA((len(segments),)),
    ]


def gemm(device, own, sib, acc, pieces, segments):
    has_acc = acc is not None
    return pl.pallas_call(
        functools.partial(gemm_body, segments, has_acc),
        in_specs=[SMEM, HBM, HBM] + [VMEM] * has_acc + [ANY] * len(pieces),
        out_specs=VMEM,
        out_shape=jax.ShapeDtypeStruct((4 * B, 2 * B), jnp.float32),
        scratch_shapes=gemm_scratch(segments),
        compiler_params=params(LIMIT),
    )(device, own, sib, *([acc] if has_acc else []), *pieces)


def finish_body(sources, segments, *refs):
    device, widths, owner, assign, weights, acc, dinv, own_inverse, sib_inverse = refs[:9]
    pieces = refs[9 : 9 + len(sources)]
    mine_out, other_out, over_out, *parts_out = refs[9 + len(sources) : 12 + len(sources) + NY]
    total, own, diag, weighted, sem, *scratch = refs[12 + len(sources) + NY :]
    last = pieces[len(sources) - len(segments) :]
    fetched = gemm_fetch(segments, device[0], own_inverse, sib_inverse, last, *scratch)
    dev, pole = device[0], device[1]
    core = dev % NC
    here_x, here_z = dev // (NZ * NC), dev // NC % NZ
    full, one, two, split = layout(widths)

    waits = []
    for j in range(2):
        block = dev if j == 0 else dev + 1 - 2 * core
        want = owner[block]
        chip, same = want // NC, want % NC == core
        for h in range(2):
            size = SIZES[h]
            target = own.at[pl.ds(j * B + h * TOP, size)]
            for piece, rows in zip(pieces, sources, strict=True):
                for at, is_same, part, (ox, oz, sided) in rows:
                    if part != h:
                        continue
                    go = oz * side(here_z, core) if sided else oz
                    here = place(here_x + ox, here_z + go, 0) // NC

                    @pl.when((here == chip) & (same == is_same))
                    def _(piece=piece, at=at, size=size, target=target, j=j, h=h):
                        pltpu.make_async_copy(
                            piece.at[pl.ds(at, size)], target, sem.at[j, h]
                        ).start()

            waits.append(
                pltpu.make_async_copy(pieces[0].at[pl.ds(0, size)], target, sem.at[j, h])
            )

    gemm_sum(fetched, acc, total, *scratch[:2])
    acc = total
    wr, wi = weights[0, assign[0]], weights[1, assign[0]]
    parts = []
    for j in range(2):
        top, low = acc[2 * j * B : (2 * j + 1) * B], acc[(2 * j + 1) * B : (2 * j + 2) * B]
        x_real = low[:, B:] - top[:, :B]
        x_imag = -(top[:, B:] + low[:, :B])
        weighted[...] = wr * x_imag + wi * x_real
        size = B // POLES
        for d in range(POLES):
            value = weighted[pl.ds(pl.multiple_of((pole ^ d) * size, size), size)]
            if d < NY:
                parts_out[d][j * size : (j + 1) * size] = value
            else:
                over_out[d - NY, j * size : (j + 1) * size] = value
        parts.append((x_real.astype(jnp.bfloat16), x_imag.astype(jnp.bfloat16)))
    for copy in waits:
        copy.wait()
    real = imag = 0
    for j in range(2):
        l_real, l_imag = own[j * B : (j + 1) * B, :B], own[j * B : (j + 1) * B, B:]
        x_real, x_imag = parts[j]
        real += transposed_dot(l_real, x_real) - transposed_dot(l_imag, x_imag)
        imag += transposed_dot(l_real, x_imag) + transposed_dot(l_imag, x_real)
    both = wr * imag + wi * real

    cut = jnp.where(core == 0, B, split)
    at_row = lax.broadcasted_iota(jnp.int32, (B, B), 0)
    at_col = lax.broadcasted_iota(jnp.int32, (B, B), 1)
    before = jnp.where((at_row < cut) & (at_col < cut), both, 0)
    after = jnp.where((at_row >= cut) & (at_col >= cut), both, 0).astype(jnp.bfloat16)
    move = moved(cut)
    after = lax.dot_general(move, after, (((1,), (0,)), ((), ())), preferred_element_type=jnp.float32)
    after = lax.dot_general(
        after.astype(jnp.bfloat16), move, (((1,), (1,)), ((), ())), preferred_element_type=jnp.float32
    )
    diag[...] = jnp.zeros_like(diag)
    first = jnp.where(core == 0, full, one)
    second = jnp.where(core == 0, one, two)
    diag[pl.ds(pl.multiple_of(first * B, B), B)] = -before
    diag[pl.ds(pl.multiple_of(second * B, B), B)] = -after
    depth = dinv.shape[1]
    mine = pl.ds(pl.multiple_of(dev * depth, 8), depth)
    diag[mine] += wr * dinv[1] + wi * dinv[0]
    for i in range(NX * NZ):
        rows = slice(i * depth, (i + 1) * depth)
        mine_out[rows] = diag[pl.ds(pl.multiple_of((NC * i + core) * depth, 8), depth)]
        total[rows, :B] = diag[pl.ds(pl.multiple_of((NC * i + 1 - core) * depth, 8), depth)]
    other_out[...] = total[: NX * NZ * depth, :B].astype(jnp.bfloat16)


def finish(
    device, widths, owner, assign, weights, acc, dinv, own, sib, pieces, sources, segments, total
):
    return pl.pallas_call(
        functools.partial(finish_body, sources, segments),
        in_specs=[SMEM] * 5 + [VMEM] * 2 + [HBM] * 2 + [ANY] * len(pieces),
        out_specs=[VMEM] * (3 + NY),
        out_shape=[
            jax.ShapeDtypeStruct((total // NC, B), jnp.float32),
            jax.ShapeDtypeStruct((total // NC, B), jnp.bfloat16),
            jax.ShapeDtypeStruct((NY, 2 * B // POLES, B), jnp.float32),
        ]
        + [jax.ShapeDtypeStruct((2 * B // POLES, B), jnp.float32)] * NY,
        scratch_shapes=[
            pltpu.VMEM((4 * B, 2 * B), jnp.float32),
            pltpu.VMEM((2 * B, 2 * B), jnp.bfloat16),
            pltpu.VMEM((total, B), jnp.float32),
            pltpu.VMEM((B, B), jnp.float32),
            pltpu.SemaphoreType.DMA((2, 2)),
            *gemm_scratch(segments),
        ],
        compiler_params=params(LIMIT),
    )(device, widths, owner, assign, weights, acc, dinv, own, sib, *pieces)


def spread_body(device, widths, got, panel, diag):
    core = device[0] % NC
    full, one, two, split = layout(widths)
    rows = B // POLES
    col = lax.broadcasted_iota(jnp.int32, (rows, B), 1)
    shares, depth = [], diag.shape[0]
    for p in range(POLES):
        out = slice(p * rows, (p + 1) * rows)
        part = got[p].astype(jnp.float32)
        mine, other = part[:rows], part[rows : 2 * rows]
        large = jnp.where(core == 0, mine, other)
        small = jnp.where(core == 0, other, mine)
        panel[out, pl.ds(pl.multiple_of(full * B, B), B)] = large
        panel[out, pl.ds(pl.multiple_of(one * B, B), B)] = jnp.where(col < split, small, 0)
        late = pltpu.roll(small, B - split, 1)
        panel[out, pl.ds(pl.multiple_of(two * B, B), B)] = jnp.where(col < B - split, late, 0)
        shares.append(part[2 * rows : 2 * rows + depth] + part[2 * rows + depth :])
    diag[...] = sum(shares)


def spread(device, widths, got, total, depth):
    return pl.pallas_call(
        spread_body,
        in_specs=[SMEM, SMEM, VMEM],
        out_specs=[VMEM, VMEM],
        out_shape=[
            jax.ShapeDtypeStruct((B, total), jnp.float32),
            jax.ShapeDtypeStruct((depth, B), jnp.float32),
        ],
        compiler_params=params(16),
    )(device, widths, got)


def local(inverse, factor, diag_inverse, widths, pattern, owner, assign, pole_weights):
    dev = lax.axis_index(GRID)
    device = jnp.stack([dev, lax.axis_index("pole")]).astype(jnp.int32)
    total = factor.shape[3]
    depth = diag_inverse.shape[2]
    own_inverse = pltpu.with_memory_space_constraint(inverse[0], pltpu.HBM)
    top, rest, give = prepare(device, in_hbm(widths), in_hbm(pattern.T), in_hbm(factor[0]))
    taken = shift(give, 0, 0, 1)
    pieces, sources = [], []

    def listing(held, offsets, kind):
        parts = ((True, TOP, B - TOP),) if kind else ((True, 0, TOP), (False, 0, B))
        segments = []
        for piece, some in zip(held, offsets, strict=True):
            rows, listed, at = [], [], 0
            for ox, oz, sided in some:
                for same, low, size in parts:
                    rows.append((ox, oz, sided, same, low, size))
                    for h, begin in enumerate((0, TOP)):
                        if low <= begin < low + size:
                            listed.append((at + begin - low, same, h, (ox, oz, sided)))
                    at += size
            pieces.append(pltpu.with_memory_space_constraint(piece, pltpu.HBM))
            sources.append(tuple(listed))
            segments.append(tuple(rows))
        return tuple(segments)

    def after(values, *others):
        values, _ = lax.optimization_barrier((values, others))
        return values

    orders = (0, -1, 1, 2)
    core = dev % NC
    rest_f, rest_b = shift(rest, 1, 0), shift(rest, -1, 0)
    main = jnp.concatenate([top, taken], 0)
    rest_f, rest_b = after((rest_f, rest_b), main)
    zf, zb = shift(main, 0, 1), shift(main, 0, -1)
    zf, zb = pass_on(zf, zb, flops=60_000_000_000)
    rest_far = shift(rest_f, 1, 0)
    main_x = after(main, rest_f, rest_b)
    main_f, main_b = shift(main_x, 1, 0), shift(main_x, -1, 0)
    across = jnp.concatenate([rest, rest_f, rest_b, rest_far], 0)
    sib_inverse = shift(after(inverse[0], main), 0, 0, 1)
    sib_inverse = pltpu.with_memory_space_constraint(sib_inverse, pltpu.HBM)
    main_far = shift(main_b, -1, 0)
    z_far = shift(zf, 0, 1)
    across_b = shift(after(across, zf, zb), 0, -1)
    zff, zbb = shift(zf, 1, 0), shift(zb, -1, 0)
    zf_late, zb_late = after((zf, zb), main_far)
    zfb, zbf = shift(zf_late, -1, 0), shift(zb_late, 1, 0)
    held = (main, main_f, main_b, main_far)
    segments = listing(held, [[(ox, 0, False)] for ox in orders], 0)
    acc = gemm(device, own_inverse, sib_inverse, None, held, segments)
    z_far, acc = after((z_far, acc), zff, zbb)
    far_f, far_b = shift(z_far, 1, 0), shift(z_far, -1, 0)
    across_f = shift(after(across, z_far), 0, 1)
    zf_far, zb_far = shift(zff, 1, 0), shift(zbb, -1, 0)
    across_far = shift(across_b, 0, -1)
    held = (zf, zff, zfb, zf_far)
    segments = listing(held, [[(ox, -1, False)] for ox in orders], 0)
    acc = gemm(device, own_inverse, sib_inverse, acc, held, segments)
    held = (zb, zbf, zbb, zb_far)
    segments = listing(held, [[(ox, 1, False)] for ox in orders], 0)
    acc = gemm(device, own_inverse, sib_inverse, acc, held, segments)
    far_f, acc = after((far_f, acc))
    far_far = shift(far_f, 1, 0)
    held, along = (z_far, far_f), (across, across_b)
    segments = listing(held, [[(0, 2, False)], [(-1, 2, False)]], 0)
    segments += listing(along, [[(ox, oz, False) for ox in orders] for oz in (0, 1)], 1)
    acc = gemm(device, own_inverse, sib_inverse, acc, held + along, segments)
    segments = listing((far_b, far_far), [[(1, 2, False)], [(2, 2, False)]], 0)
    along = (across_f, across_far)
    segments += listing(along, [[(ox, oz, False) for ox in orders] for oz in (-1, 2)], 1)

    mine, given, over, *parts = finish(
        device, in_hbm(widths), in_hbm(owner), assign, in_hbm(pole_weights.T), acc,
        diag_inverse[0].astype(jnp.float32), own_inverse, sib_inverse,
        pieces, tuple(sources), segments, total,
    )

    mine = mine + shift(given, 0, 0, 1).astype(jnp.float32)
    mine = mine.reshape(NX * NZ, depth, B)
    groups = [[NC * i + c for i in range(NX * NZ)] for c in range(NC)]
    shared = lax.all_to_all(mine, GRID, 0, 0, axis_index_groups=groups, tiled=True)
    over = lax.ppermute(over, "pole", [(p, p ^ NY) for p in range(POLES)])
    got = [part + over[d] for d, part in enumerate(parts)]
    got = [
        lax.ppermute(part, "pole", [(p, p ^ d) for p in range(POLES)]) if d else part
        for d, part in enumerate(got)
    ]
    got = sum(got).astype(jnp.bfloat16)
    rows = B // POLES
    other = shift(got[rows:], 0, 0, 1)
    diag = shared.astype(jnp.float32).sum(0)
    high = diag.astype(jnp.bfloat16)
    low = (diag - high.astype(jnp.float32)).astype(jnp.bfloat16)
    both = jnp.concatenate([got[:rows], other, high, low], 0)
    both = lax.all_to_all(
        jnp.broadcast_to(both[None], (POLES,) + both.shape), "pole", 0, 0, tiled=True
    )
    return tuple(spread(device, widths, both, total, depth))


def solution(mesh):
    placed = (
        P("pole", None, None, GRID),
        P("pole", None, GRID, None),
        P("pole", None, GRID, None),
        P(),
        P(),
        P(),
        P("pole"),
        P(),
    )
    return jax.shard_map(
        local,
        mesh=mesh,
        in_specs=placed,
        out_specs=(P(GRID, None), P(GRID, None)),
        check_vma=False,
    )
```
